256 devices in a mesh: dist: 64 (over z, y, core), rep: 4 (over x).
Axes of the slice: x: 4, y: 4, z: 8, core: 2. Of those that a mesh axis runs over, the one named last changes fastest.
Arguments:
- amplitudes: float32 [2816, 19200], P(None, 'dist'), may hold values from -6 to 6
- integrals: float32 [2816, 19200], P('dist', 'rep'), may hold values from -0.3125 to 0.3125
- slab_irrep: int32 [176], replicated, may hold values from 0 to 7, as said below
- virtual_irrep: int32 [1200], replicated, may hold values from 0 to 7, as said below
- occupied_irrep: int32 [16], replicated, may hold values from 0 to 7, as said below
- occupied_energy: float32 [16], replicated, may hold values from -2 to -0.5
- slab_energy: float32 [176], replicated, may hold values from 0.2 to 3
Outputs:
- update: float32 [2816, 2816], P('rep', 'dist')
The draws below stay inside these ranges and needn't reach their ends.
Inputs may be any that keep to these rules, and one draw needn't show every extreme that they name: `slab_irrep`: labels do not fall along the slab; every one of the 8 irreps labels at least 11 slab orbitals. `virtual_irrep`: labels do not fall along the virtual orbitals; every one of the 8 irreps labels at least 75 virtual orbitals. `occupied_irrep`: every irrep labels exactly 2 occupied orbitals.
All inputs are finite; a program needn't handle non-finite values.
Results may differ from the reference program's by a relative error of at most 0.000084.
Values sent between devices are 32-bit elements; how exact they have to be, the bound alone decides.
A program may use at most 64 MiB of HBM per device.

```python
import math
import jax
import jax.numpy as jnp
from jax import lax

V = 1200
AS = 176
O = 16
M = 2816
K = 19200


def sorted_labels(key, count, least):
    cuts = jnp.sort(jax.random.randint(key, (7,), 0, count - 8 * least + 1))
    bounds = least * jnp.arange(1, 8, dtype=jnp.int32) + cuts
    places = jnp.arange(count, dtype=jnp.int32)
    return jnp.sum((places[:, None] >= bounds[None, :]).astype(jnp.int32), axis=1).astype(jnp.int32)


def draw_slab_irrep(key, part):
    key = jax.random.fold_in(key, 11)
    return sorted_labels(key, AS, AS // 16)


def draw_virtual_irrep(key, part):
    key = jax.random.fold_in(key, 12)
    return sorted_labels(key, V, V // 16)


def draw_occupied_irrep(key, part):
    key = jax.random.fold_in(key, 13)
    return (jax.random.permutation(key, O) % 8).astype(jnp.int32)


def raised(drawn, rng, source, target, shards_of, factor):
    owner, partner = [(jnp.arange(drawn.shape[dim]) // (drawn.shape[dim] // shards_of)).reshape([-1 if axis == dim else 1 for axis in range(drawn.ndim)]) for dim in (source, target)]
    chosen = jax.random.permutation(rng, shards_of)[partner]
    strong = (owner == chosen) | (owner == (partner + shards_of // 2) % shards_of)
    return jnp.where(strong, factor * drawn, drawn)


def shard_levels(own_key, extent, shards, low, largest):
    gain, own = 1.0, jax.random.fold_in(own_key, 6)
    for position, blocks in shards:
        draws = jnp.exp(jax.random.uniform(jax.random.fold_in(own, position), (blocks,), jnp.float32, low / len(shards), largest / len(shards)))
        gain = gain * jnp.repeat(draws, extent[position] // blocks).reshape([-1 if axis == position else 1 for axis in range(len(extent))])
    return gain


def centred(own_key, extent, spread, bound, shards=(), kind=jnp.bfloat16):
    factor_of = shard_levels(own_key, extent, shards, -0.22, 0.18) if shards else 1.0
    result = jax.random.normal(own_key, extent, jnp.float32) * spread * factor_of
    return jnp.minimum(jnp.maximum(result, -bound), bound).astype(kind)


def gaussian_with(own_key, shape, spread, reach, cuts, heavy, kind=jnp.bfloat16):
    array = spread * jax.random.normal(own_key, shape, jnp.float32)
    if cuts:
        array = array * shard_levels(own_key, shape, cuts, -0.22, 0.18)
    return jnp.clip(raised(array, jax.random.fold_in(own_key, 3), *heavy), -reach, reach).astype(kind)


def setup_inputs(seed: int = 0) -> dict:
    arg_keys = jax.random.split(jax.random.key(seed), 8)
    return {
        "amplitudes": centred(arg_keys[0], (M, K), 1.0, 6.0, ((1, 64),), jnp.float32),
        "integrals": gaussian_with(arg_keys[1], (M, K), (K // 8) ** -0.5, 0.3125, ((0, 64), (1, 4)), (1, 0, 64, 4.0), jnp.float32),
        "slab_irrep": draw_slab_irrep(jax.random.fold_in(arg_keys[7], 71), 0),
        "virtual_irrep": draw_virtual_irrep(jax.random.fold_in(arg_keys[7], 71), 0),
        "occupied_irrep": draw_occupied_irrep(jax.random.fold_in(arg_keys[7], 71), 0),
        "occupied_energy": jnp.clip(jax.random.uniform(arg_keys[5], (O,), jnp.float32, -2.0, -0.5), -2.0, -0.5),
        "slab_energy": jnp.clip(jnp.exp(jax.random.uniform(arg_keys[6], (AS,), jnp.float32, math.log(0.2), math.log(3.0))), 0.2, 3.0),
    }


def reference(amplitudes, integrals, slab_irrep, virtual_irrep, occupied_irrep, occupied_energy, slab_energy):
    row_symmetry = jnp.bitwise_xor(slab_irrep[:, None], occupied_irrep[None, :]).reshape(-1)
    col_symmetry = jnp.bitwise_xor(virtual_irrep[:, None], occupied_irrep[None, :]).reshape(-1)
    allowed = row_symmetry[:, None] == col_symmetry[None, :]
    amp_masked = jnp.where(allowed, amplitudes, jnp.float32(0.0))
    int_masked = jnp.where(allowed, integrals, jnp.float32(0.0))
    cycle = lax.dot_general(amp_masked, int_masked, (((1,), (1,)), ((), ())),
                           precision=lax.Precision.HIGHEST, preferred_element_type=jnp.float32)
    shifts = (occupied_energy[None, :] - slab_energy[:, None]).reshape(-1)
    return cycle / (shifts[:, None] + shifts[None, :])
```

```python
import jax
import jax.numpy as jnp
from jax import lax
from jax.experimental import pallas as pl
from jax.experimental.pallas import tpu as pltpu
from jax.sharding import PartitionSpec as P

MESH = pl.DeviceIdType.MESH
F32, BF16, I32 = jnp.float32, jnp.bfloat16, jnp.int32

O = 16
IRREPS = 8
Z, Y, X = 8, 4, 4
PLACES = 8
ROWS = 2816
COLS = 300
WIDE = 4800
HALF = 2400
BJ = 44
MY = 704
SLOTS = 40
QA = 88
APAD, BPAD = 304, 48
START = [(COLS * p) // O for p in range(PLACES)]


def halves(value):
    high = value.astype(BF16)
    return high, (value - high.astype(F32)).astype(BF16)


def matmul(left, right, dims):
    return lax.dot_general(left, right, (dims, ((), ())), preferred_element_type=F32)


NN = ((1,), (0,))
NT = ((1,), (1,))


def kernel(
    a_hbm,
    w_hbm,
    row_sym,
    a_col_sym,
    w_col_sym,
    bj_sym,
    a_code,
    bj_code,
    bj_code_col,
    rank_key,
    out_sym,
    out_shift,
    bj_shift,
    out_ref,
    a_in,
    w_in,
    a_split,
    w_split,
    pick,
    a_msg,
    w_msg,
    a_got,
    w_got,
    a_all,
    o_msg,
    o_got,
    load_sem,
    a_send,
    w_send,
    o_send,
    a_recv,
    w_recv,
    o_recv,
):
    d = lax.axis_index("dist")
    x = lax.axis_index("rep")
    z, place = d // PLACES, d % PLACES
    y, core = place // 2, place % 2
    home_y = (x - y + Y) % Y
    self_w = jnp.where((z // 2 == x) & (home_y == y), 1, 0)
    self_o = jnp.where(home_y == y, 1, 0)

    load_a = pltpu.make_async_copy(a_hbm, a_in, load_sem.at[0])
    load_w = pltpu.make_async_copy(w_hbm, w_in, load_sem.at[1])
    load_w.start()
    load_a.start()

    barrier = pltpu.get_barrier_semaphore()

    def greet(dd, xx):
        pl.semaphore_signal(barrier, inc=1, device_id=(dd, xx), device_id_type=MESH)

    def greet_a(i, carry):
        greet(z * PLACES + (place + i) % PLACES, x)
        return carry

    def greet_w(i, carry):
        zs = (z + i // 2) % Z
        cs = i % 2
        dd, xx = zs * PLACES + home_y * 2 + cs, z // 2

        @pl.when(jnp.logical_not((dd == d) & (xx == x)))
        def _():
            greet(dd, xx)

        return carry

    def greet_o(i, carry):
        zs = (z + i // PLACES) % Z
        s = (place + i) % PLACES
        dd, xx = zs * PLACES + s, (y + s // 2) % Y

        @pl.when(jnp.logical_not((dd == d) & (xx == x)))
        def _():
            greet(dd, xx)

        return carry

    lax.fori_loop(1, PLACES, greet_a, 0)
    lax.fori_loop(0, 2 * Z, greet_w, 0)
    lax.fori_loop(0, Z * PLACES, greet_o, 0)

    for n in range(8):
        cols = pl.ds(n * 256, 256)
        slot = lax.broadcasted_iota(I32, (256, 256), 0)
        pick[:, cols] = (rank_key[:, cols] == slot).astype(F32).astype(BF16)
    for n in range(4):
        o_msg[n] = jnp.zeros((2 * Z, 8, 128), F32)
        w_split[pl.ds(n * BPAD + 32, 16)] = jnp.zeros((16, 2432), BF16)
    for n in range(2):
        a_split[pl.ds(n * APAD + 288, 16)] = jnp.zeros((16, ROWS), BF16)

    load_w.wait()
    for half in range(2):
        cols = pl.ds(half * HALF, HALF)
        kept = jnp.where(bj_sym[pl.ds(0, BJ)] == w_col_sym[:, cols], w_in[:, cols], 0.0)
        high, low = halves(kept)
        w_split[pl.ds(half * 2 * BPAD, BJ), pl.ds(0, HALF)] = high
        w_split[pl.ds((half * 2 + 1) * BPAD, BJ), pl.ds(0, HALF)] = low
    w_main = matmul(w_split[:, pl.ds(0, 2048)], pick[...], NT)
    w_rest = matmul(
        w_split[:, pl.ds(2048, HALF - 2048)], pick[pl.ds(0, 128), pl.ds(0, HALF - 2048)], NT
    )
    group = lax.broadcasted_iota(I32, (IRREPS * 8, 2 * BPAD), 0) == bj_code[...]
    group = group.astype(F32).astype(BF16)
    for half in range(2):
        rows = slice(half * 2 * BPAD, (half + 1) * 2 * BPAD)
        main = matmul(group, w_main[rows].astype(BF16), NN)
        rest = matmul(group, w_rest[rows].astype(BF16), NN)
        w_msg[half, :, :, pl.ds(0, 256)] = main.reshape(IRREPS, 8, 256)
        w_msg[half, :, :, pl.ds(256, 128)] = rest.reshape(IRREPS, 8, 128)

    pl.semaphore_wait(barrier, 7 + 2 * Z - self_w + Z * PLACES - self_o)

    slot_w = z * 2 + core

    def w_route(i):
        half = i // PLACES
        s = (place + i) % PLACES
        dd, xx = (2 * x + half) * PLACES + s, (y + s // 2) % Y
        return half, s, dd, xx, (dd == d) & (xx == x)

    def w_copy(i):
        half, s, dd, xx, _ = w_route(i)
        return pltpu.make_async_remote_copy(
            src_ref=w_msg.at[half, s],
            dst_ref=w_got.at[slot_w],
            send_sem=w_send.at[i],
            recv_sem=w_recv,
            device_id=(dd, xx),
            device_id_type=MESH,
        )

    def send_w(i, carry):
        half, s, dd, xx, mine = w_route(i)

        @pl.when(mine)
        def _():
            pltpu.make_async_copy(w_msg.at[half, s], w_got.at[slot_w], w_recv).start()

        @pl.when(jnp.logical_not(mine))
        def _():
            w_copy(i).start()

        return carry

    lax.fori_loop(0, 2 * PLACES, send_w, 0)

    load_a.wait()
    for n in range(11):
        cols = pl.ds(n * 256, 256)
        kept = jnp.where(a_col_sym[...] == row_sym[:, cols], a_in[:, cols], 0.0)
        high, low = halves(kept)
        a_split[pl.ds(0, COLS), cols] = high
        a_split[pl.ds(APAD, COLS), cols] = low
    a_main = matmul(a_split[:, pl.ds(0, 2048)], pick[...], NT)
    a_rest = matmul(
        a_split[:, pl.ds(2048, ROWS - 2048)], pick[pl.ds(0, 128), pl.ds(0, ROWS - 2048)], NT
    )
    place_rows = lax.broadcasted_iota(I32, (IRREPS * SLOTS, 2 * APAD), 0) == a_code[...]
    place_rows = place_rows.astype(F32).astype(BF16)
    main = matmul(place_rows, a_main.astype(BF16), NN)
    rest = matmul(place_rows, a_rest.astype(BF16), NN)
    a_msg[:, :, pl.ds(0, 256)] = main.reshape(IRREPS, SLOTS, 256)
    a_msg[:, :, pl.ds(256, 128)] = rest.reshape(IRREPS, SLOTS, 128)

    def a_copy(i):
        s = (place + i) % PLACES
        return pltpu.make_async_remote_copy(
            src_ref=a_msg.at[s],
            dst_ref=a_got.at[place],
            send_sem=a_send.at[i],
            recv_sem=a_recv,
            device_id=(z * PLACES + s, x),
            device_id_type=MESH,
        )

    def send_a(i, carry):
        a_copy(i).start()
        return carry

    lax.fori_loop(1, PLACES, send_a, 0)
    pltpu.make_async_copy(a_msg.at[place], a_got.at[place], a_recv).start()

    a_all[...] = jnp.zeros(a_all.shape, F32)
    pltpu.make_async_copy(a_got, a_got, a_recv).wait()
    for p in range(PLACES):
        first = 2 * START[p]
        a_all[pl.ds(first, SLOTS), :] += a_got[p]
    pltpu.make_async_copy(w_got, w_got, w_recv).wait()
    w_high, w_low = halves(w_got[...].reshape(2 * Z * 8, 384))
    a_high, a_low = halves(a_all[...])
    product = matmul(w_high, a_low, NN) + matmul(w_low, a_high, NN)
    product = product + matmul(w_high, a_high, NN)
    for part in range(X):
        o_msg[part, :, :, pl.ds(0, QA)] = product[:, part * QA : (part + 1) * QA].reshape(
            2 * Z, 8, QA
        )

    def o_route(i):
        zs = (z + i // PLACES) % Z
        cs = (core + i) % 2
        part = (x + (i % PLACES) // 2) % X
        dd = zs * PLACES + home_y * 2 + cs
        return zs * 2 + cs, part, dd, (dd == d) & (part == x)

    def o_copy(i):
        w, part, dd, _ = o_route(i)
        return pltpu.make_async_remote_copy(
            src_ref=o_msg.at[part, w],
            dst_ref=o_got.at[d],
            send_sem=o_send.at[i],
            recv_sem=o_recv,
            device_id=(dd, part),
            device_id_type=MESH,
        )

    def send_o(i, carry):
        w, part, dd, mine = o_route(i)

        @pl.when(mine)
        def _():
            pltpu.make_async_copy(o_msg.at[part, w], o_got.at[d], o_recv).start()

        @pl.when(jnp.logical_not(mine))
        def _():
            o_copy(i).start()

        return carry

    lax.fori_loop(0, Z * PLACES, send_o, 0)

    spread = (
        lax.broadcasted_iota(I32, (BPAD, 128), 1) % 64 == bj_code_col[...]
    ).astype(F32).astype(BF16)
    pltpu.make_async_copy(o_got, o_got, o_recv).wait()
    total = o_got[pl.ds(0, PLACES)]
    for zs in range(1, Z):
        total = total + o_got[pl.ds(zs * PLACES, PLACES)]
    high, low = halves(total.reshape(IRREPS * 8, 128))
    mine = matmul(spread, jnp.concatenate([high, low], axis=0), NN)
    high, low = halves(mine)
    widen = pick[pl.ds(0, 128), pl.ds(0, MY)]
    cycle = matmul(high, widen, NN) + matmul(low, widen, NN)
    value = jnp.where(bj_sym[...] == out_sym[...], cycle, 0.0) / (out_shift[...] + bj_shift[...])
    out_ref[...] = value[:BJ]

    def done_w(i, carry):
        @pl.when(jnp.logical_not(w_route(i)[4]))
        def _():
            w_copy(i).wait_send()

        return carry

    def done_a(i, carry):
        a_copy(i).wait_send()
        return carry

    def done_o(i, carry):
        @pl.when(jnp.logical_not(o_route(i)[3]))
        def _():
            o_copy(i).wait_send()

        return carry

    lax.fori_loop(0, 2 * PLACES, done_w, 0)
    lax.fori_loop(1, PLACES, done_a, 0)
    lax.fori_loop(0, Z * PLACES, done_o, 0)


def local(
    amplitudes, integrals, slab_irrep, virtual_irrep, occupied_irrep, occupied_energy, slab_energy
):
    d = lax.axis_index("dist")
    x = lax.axis_index("rep")
    row_sym = (slab_irrep[:, None] ^ occupied_irrep[None, :]).reshape(-1)
    col_sym = (virtual_irrep[:, None] ^ occupied_irrep[None, :]).reshape(-1)
    shifts = (occupied_energy[None, :] - slab_energy[:, None]).reshape(-1)
    same = occupied_irrep[:, None] == occupied_irrep[None, :]
    earlier = jnp.arange(O)[None, :] < jnp.arange(O)[:, None]
    rank = jnp.sum((same & earlier).astype(I32), axis=1)

    a_sym = lax.dynamic_slice_in_dim(col_sym, d * COLS, COLS, 0)
    w_sym = lax.dynamic_slice_in_dim(col_sym, x * WIDE, WIDE, 0)
    bj_sym = lax.dynamic_slice_in_dim(row_sym, d * BJ, BJ, 0)
    out_sym = lax.dynamic_slice_in_dim(row_sym, x * MY, MY, 0)
    bj_shift = lax.dynamic_slice_in_dim(shifts, d * BJ, BJ, 0)
    out_shift = lax.dynamic_slice_in_dim(shifts, x * MY, MY, 0)

    position = (d % PLACES) * COLS + jnp.arange(COLS)
    ranks = jnp.tile(rank, 128)
    my_rank = lax.dynamic_slice_in_dim(jnp.tile(rank, 20), (d * COLS) % O, COLS, 0)
    a_slot = 2 * (position // O - ((d % PLACES) * COLS) // O) + my_rank
    a_code = SLOTS * a_sym + a_slot
    a_code = jnp.pad(a_code, (0, APAD - COLS), constant_values=-1)
    before = jnp.arange(BJ)[None, :] < jnp.arange(BJ)[:, None]
    bj_slot = jnp.sum(((bj_sym[:, None] == bj_sym[None, :]) & before).astype(I32), axis=1)
    bj_code = jnp.pad(8 * bj_sym + bj_slot, (0, BPAD - BJ), constant_values=-1)
    rank_key = 2 * (jnp.arange(2048) // O) + ranks

    def pad(v, size, value):
        return jnp.pad(v, (0, size - v.shape[0]), constant_values=value)

    vmem = pl.BlockSpec(memory_space=pltpu.VMEM)
    hbm = pl.BlockSpec(memory_space=pl.ANY)
    out = pl.pallas_call(
        kernel,
        out_shape=jax.ShapeDtypeStruct((BJ, MY), F32),
        in_specs=[hbm, hbm] + [vmem] * 11,
        out_specs=vmem,
        scratch_shapes=[
            pltpu.VMEM((COLS, ROWS), F32),
            pltpu.VMEM((BJ, WIDE), F32),
            pltpu.VMEM((2 * APAD, ROWS), BF16),
            pltpu.VMEM((4 * BPAD, 2432), BF16),
            pltpu.VMEM((256, 2048), BF16),
            pltpu.VMEM((IRREPS, SLOTS, 384), F32),
            pltpu.VMEM((2, IRREPS, 8, 384), F32),
            pltpu.VMEM((PLACES, SLOTS, 384), F32),
            pltpu.VMEM((2 * Z, 8, 384), F32),
            pltpu.VMEM((384, 384), F32),
            pltpu.VMEM((X, 2 * Z, 8, 128), F32),
            pltpu.VMEM((Z * PLACES, 8, 128), F32),
            pltpu.SemaphoreType.DMA((2,)),
            pltpu.SemaphoreType.DMA((PLACES,)),
            pltpu.SemaphoreType.DMA((2 * PLACES,)),
            pltpu.SemaphoreType.DMA((Z * PLACES,)),
            pltpu.SemaphoreType.DMA,
            pltpu.SemaphoreType.DMA,
            pltpu.SemaphoreType.DMA,
        ],
        compiler_params=pltpu.CompilerParams(
            collective_id=0, has_side_effects=True, vmem_limit_bytes=48 * 1024 * 1024
        ),
    )(
        amplitudes.T,
        integrals,
        row_sym[None, :],
        a_sym[:, None],
        w_sym[None, :],
        pad(bj_sym, BPAD, -1)[:, None],
        jnp.concatenate([a_code, a_code])[None, :],
        jnp.concatenate([bj_code, bj_code])[None, :],
        bj_code[:, None],
        rank_key[None, :],
        out_sym[None, :],
        out_shift[None, :],
        pad(bj_shift, BPAD, 1.0)[:, None],
    )
    return out.T


def solution(mesh):
    return jax.shard_map(
        local,
        mesh=mesh,
        in_specs=(P(None, "dist"), P("dist", "rep"), P(), P(), P(), P(), P()),
        out_specs=P("rep", "dist"),
        check_vma=False,
    )
```

```python
import jax
import jax.numpy as jnp
from jax import lax
from jax.experimental import pallas as pl
from jax.experimental.pallas import tpu as pltpu
from jax.sharding import PartitionSpec as P

MESH = pl.DeviceIdType.MESH
F32, BF16, I32 = jnp.float32, jnp.bfloat16, jnp.int32

O = 16
IRREPS = 8
Z, Y, X = 8, 4, 4
PLACES = 8
ROWS = 2816
COLS = 300
WIDE = 4800
HALF = 2400
BJ = 44
MY = 704
SLOTS = 40
QA = 88
APAD, BPAD = 304, 48
START = [(COLS * p) // O for p in range(PLACES)]


def halves(value):
    high = value.astype(BF16)
    return high, (value - high.astype(F32)).astype(BF16)


def matmul(left, right, dims):
    return lax.dot_general(left, right, (dims, ((), ())), preferred_element_type=F32)


NN = ((1,), (0,))
NT = ((1,), (1,))


def kernel(
    a_hbm,
    w_hbm,
    row_sym,
    a_col_sym,
    w_col_sym,
    bj_sym,
    a_code,
    bj_code,
    bj_code_col,
    rank_key,
    out_sym,
    out_shift,
    bj_shift,
    out_ref,
    a_in,
    w_in,
    a_split,
    w_split,
    pick,
    a_msg,
    w_msg,
    w_mid,
    a_got,
    w_got,
    a_all,
    o_msg,
    o_got,
    load_sem,
    a_send,
    x_send,
    w_send,
    o_send,
    a_recv,
    x_recv,
    w_recv,
    o_recv,
):
    d = lax.axis_index("dist")
    x = lax.axis_index("rep")
    z, place = d // PLACES, d % PLACES
    y, core = place // 2, place % 2
    load_a = pltpu.make_async_copy(a_hbm, a_in, load_sem.at[0])
    load_w = pltpu.make_async_copy(w_hbm, w_in, load_sem.at[1])
    load_w.start()
    load_a.start()

    barrier = pltpu.get_barrier_semaphore()

    def greet(dd, xx):
        pl.semaphore_signal(barrier, inc=1, device_id=(dd, xx), device_id_type=MESH)

    def greet_a(i, carry):
        greet(z * PLACES + (place + i) % PLACES, x)
        return carry

    def greet_o(i, carry):
        zs, cs, xs = (z + i // PLACES) % Z, (core + i) % 2, (x + (i % PLACES) // 2) % X
        greet(zs * PLACES + y * 2 + cs, xs)
        return carry

    lax.fori_loop(2 - core, PLACES - core, greet_a, 0)
    lax.fori_loop(1, Z * PLACES, greet_o, 0)

    for n in range(8):
        cols = pl.ds(n * 256, 256)
        slot = lax.broadcasted_iota(I32, (256, 256), 0)
        pick[:, cols] = (rank_key[:, cols] == slot).astype(F32).astype(BF16)
    for n in range(4):
        o_msg[n] = jnp.zeros((2 * Z, 8, 128), F32)
        w_split[pl.ds(n * BPAD + 32, 16)] = jnp.zeros((16, 2432), BF16)
    for n in range(2):
        a_split[pl.ds(n * APAD + 288, 16)] = jnp.zeros((16, ROWS), BF16)

    load_w.wait()
    for half in range(2):
        cols = pl.ds(half * HALF, HALF)
        kept = jnp.where(bj_sym[pl.ds(0, BJ)] == w_col_sym[:, cols], w_in[:, cols], 0.0)
        high, low = halves(kept)
        w_split[pl.ds(half * 2 * BPAD, BJ), pl.ds(0, HALF)] = high
        w_split[pl.ds((half * 2 + 1) * BPAD, BJ), pl.ds(0, HALF)] = low
    w_main = matmul(w_split[:, pl.ds(0, 2048)], pick[...], NT)
    w_rest = matmul(
        w_split[:, pl.ds(2048, HALF - 2048)], pick[pl.ds(0, 128), pl.ds(0, HALF - 2048)], NT
    )
    group = lax.broadcasted_iota(I32, (IRREPS * 8, 2 * BPAD), 0) == bj_code[...]
    group = group.astype(F32).astype(BF16)
    for half in range(2):
        rows = slice(half * 2 * BPAD, (half + 1) * 2 * BPAD)
        main = matmul(group, w_main[rows].astype(BF16), NN)
        rest = matmul(group, w_rest[rows].astype(BF16), NN)
        w_msg[:, half, :, pl.ds(0, 256)] = main.reshape(IRREPS, 8, 256)
        w_msg[:, half, :, pl.ds(256, 128)] = rest.reshape(IRREPS, 8, 128)

    pl.semaphore_wait(barrier, 6 + Z * PLACES - 1)

    def x_copy(i):
        cs, xs = (core + i // 3) % 2, (x + 1 + i % 3) % X
        return pltpu.make_async_remote_copy(
            src_ref=w_msg.at[2 * xs + cs],
            dst_ref=w_mid.at[cs, x],
            send_sem=x_send.at[i],
            recv_sem=x_recv.at[cs],
            device_id=(d, xs),
            device_id_type=MESH,
        )

    def send_x(i, carry):
        x_copy(i).start()
        return carry

    lax.fori_loop(0, 6, send_x, 0)
    for cs in range(2):
        pltpu.make_async_copy(w_msg.at[2 * x + cs], w_mid.at[cs, x], x_recv.at[cs]).start()

    load_a.wait()
    for n in range(11):
        cols = pl.ds(n * 256, 256)
        kept = jnp.where(a_col_sym[...] == row_sym[:, cols], a_in[:, cols], 0.0)
        high, low = halves(kept)
        a_split[pl.ds(0, COLS), cols] = high
        a_split[pl.ds(APAD, COLS), cols] = low
    a_main = matmul(a_split[:, pl.ds(0, 2048)], pick[...], NT)
    a_rest = matmul(
        a_split[:, pl.ds(2048, ROWS - 2048)], pick[pl.ds(0, 128), pl.ds(0, ROWS - 2048)], NT
    )
    place_rows = lax.broadcasted_iota(I32, (2 * SLOTS, 2 * APAD), 0) == (
        a_code[...] - 2 * SLOTS * x
    )
    place_rows = place_rows.astype(F32).astype(BF16)
    main = matmul(place_rows, a_main.astype(BF16), NN)
    rest = matmul(place_rows, a_rest.astype(BF16), NN)
    a_msg[:, :, pl.ds(0, 256)] = main.reshape(2, SLOTS, 256)
    a_msg[:, :, pl.ds(256, 128)] = rest.reshape(2, SLOTS, 128)

    def a_copy(i):
        to = (place + i) % PLACES
        return pltpu.make_async_remote_copy(
            src_ref=a_msg.at[to % 2],
            dst_ref=a_got.at[place],
            send_sem=a_send.at[i],
            recv_sem=a_recv,
            device_id=(z * PLACES + to, x),
            device_id_type=MESH,
        )

    def send_a(i, carry):
        a_copy(i).start()
        return carry

    lax.fori_loop(1, PLACES, send_a, 0)
    pltpu.make_async_copy(a_msg.at[core], a_got.at[place], a_recv).start()

    slot_w = z * 2 + core

    def w_copy(i):
        cs, zs = (core + i // Z) % 2, (z + i) % Z
        return pltpu.make_async_remote_copy(
            src_ref=w_mid.at[cs, zs // 2, zs % 2],
            dst_ref=w_got.at[slot_w],
            send_sem=w_send.at[i],
            recv_sem=w_recv,
            device_id=(zs * PLACES + y * 2 + cs, x),
            device_id_type=MESH,
        )

    def send_w(i, carry):
        w_copy(i).start()
        return carry

    first, second = w_mid.at[core], w_mid.at[1 - core]
    pltpu.make_async_copy(first, first, x_recv.at[core]).wait()
    pltpu.make_async_copy(first.at[z // 2, z % 2], w_got.at[slot_w], w_recv).start()
    lax.fori_loop(1, Z, send_w, 0)
    pltpu.make_async_copy(second, second, x_recv.at[1 - core]).wait()
    lax.fori_loop(Z, 2 * Z, send_w, 0)

    a_all[...] = jnp.zeros(a_all.shape, F32)
    pltpu.make_async_copy(a_got, a_got, a_recv).wait()
    for p in range(PLACES):
        first = 2 * START[p]
        a_all[pl.ds(first, SLOTS), :] += a_got[p]
    pltpu.make_async_copy(w_got, w_got, w_recv).wait()
    w_high, w_low = halves(w_got[...].reshape(2 * Z * 8, 384))
    a_high, a_low = halves(a_all[...])
    product = matmul(w_high, a_low, NN) + matmul(w_low, a_high, NN)
    product = product + matmul(w_high, a_high, NN)
    for part in range(X):
        o_msg[part, :, :, pl.ds(0, QA)] = product[:, part * QA : (part + 1) * QA].reshape(
            2 * Z, 8, QA
        )

    def o_copy(i):
        zs, cs, part = (z + i // PLACES) % Z, (core + i) % 2, (x + (i % PLACES) // 2) % X
        return pltpu.make_async_remote_copy(
            src_ref=o_msg.at[part, zs * 2 + cs],
            dst_ref=o_got.at[z * PLACES + 2 * x + core],
            send_sem=o_send.at[i],
            recv_sem=o_recv,
            device_id=(zs * PLACES + y * 2 + cs, part),
            device_id_type=MESH,
        )

    def send_o(i, carry):
        o_copy(i).start()
        return carry

    lax.fori_loop(1, Z * PLACES, send_o, 0)
    pltpu.make_async_copy(
        o_msg.at[x, slot_w], o_got.at[z * PLACES + 2 * x + core], o_recv
    ).start()

    spread = (
        lax.broadcasted_iota(I32, (BPAD, 128), 1) % 64 == bj_code_col[...]
    ).astype(F32).astype(BF16)
    pltpu.make_async_copy(o_got, o_got, o_recv).wait()
    total = o_got[pl.ds(0, PLACES)]
    for zs in range(1, Z):
        total = total + o_got[pl.ds(zs * PLACES, PLACES)]
    high, low = halves(total.reshape(IRREPS * 8, 128))
    mine = matmul(spread, jnp.concatenate([high, low], axis=0), NN)
    high, low = halves(mine)
    widen = pick[pl.ds(0, 128), pl.ds(0, MY)]
    cycle = matmul(high, widen, NN) + matmul(low, widen, NN)
    value = jnp.where(bj_sym[...] == out_sym[...], cycle, 0.0) / (out_shift[...] + bj_shift[...])
    out_ref[...] = value[:BJ]

    def done_x(i, carry):
        x_copy(i).wait_send()
        return carry

    def done_w(i, carry):
        w_copy(i).wait_send()
        return carry

    def done_a(i, carry):
        a_copy(i).wait_send()
        return carry

    def done_o(i, carry):
        o_copy(i).wait_send()
        return carry

    lax.fori_loop(0, 6, done_x, 0)
    lax.fori_loop(1, 2 * Z, done_w, 0)
    lax.fori_loop(1, PLACES, done_a, 0)
    lax.fori_loop(1, Z * PLACES, done_o, 0)


def local(
    amplitudes, integrals, slab_irrep, virtual_irrep, occupied_irrep, occupied_energy, slab_energy
):
    d = lax.axis_index("dist")
    x = lax.axis_index("rep")
    row_sym = (slab_irrep[:, None] ^ occupied_irrep[None, :]).reshape(-1)
    col_sym = (virtual_irrep[:, None] ^ occupied_irrep[None, :]).reshape(-1)
    shifts = (occupied_energy[None, :] - slab_energy[:, None]).reshape(-1)
    same = occupied_irrep[:, None] == occupied_irrep[None, :]
    earlier = jnp.arange(O)[None, :] < jnp.arange(O)[:, None]
    rank = jnp.sum((same & earlier).astype(I32), axis=1)

    a_sym = lax.dynamic_slice_in_dim(col_sym, d * COLS, COLS, 0)
    w_sym = lax.dynamic_slice_in_dim(col_sym, x * WIDE, WIDE, 0)
    bj_sym = lax.dynamic_slice_in_dim(row_sym, d * BJ, BJ, 0)
    out_sym = lax.dynamic_slice_in_dim(row_sym, x * MY, MY, 0)
    bj_shift = lax.dynamic_slice_in_dim(shifts, d * BJ, BJ, 0)
    out_shift = lax.dynamic_slice_in_dim(shifts, x * MY, MY, 0)

    position = (d % PLACES) * COLS + jnp.arange(COLS)
    ranks = jnp.tile(rank, 128)
    my_rank = lax.dynamic_slice_in_dim(jnp.tile(rank, 20), (d * COLS) % O, COLS, 0)
    a_slot = 2 * (position // O - ((d % PLACES) * COLS) // O) + my_rank
    a_code = SLOTS * a_sym + a_slot
    a_code = jnp.pad(a_code, (0, APAD - COLS), constant_values=-1)
    before = jnp.arange(BJ)[None, :] < jnp.arange(BJ)[:, None]
    bj_slot = jnp.sum(((bj_sym[:, None] == bj_sym[None, :]) & before).astype(I32), axis=1)
    bj_code = jnp.pad(8 * bj_sym + bj_slot, (0, BPAD - BJ), constant_values=-1)
    rank_key = 2 * (jnp.arange(2048) // O) + ranks

    def pad(v, size, value):
        return jnp.pad(v, (0, size - v.shape[0]), constant_values=value)

    vmem = pl.BlockSpec(memory_space=pltpu.VMEM)
    hbm = pl.BlockSpec(memory_space=pl.ANY)
    out = pl.pallas_call(
        kernel,
        out_shape=jax.ShapeDtypeStruct((BJ, MY), F32),
        in_specs=[hbm, hbm] + [vmem] * 11,
        out_specs=vmem,
        scratch_shapes=[
            pltpu.VMEM((COLS, ROWS), F32),
            pltpu.VMEM((BJ, WIDE), F32),
            pltpu.VMEM((2 * APAD, ROWS), BF16),
            pltpu.VMEM((4 * BPAD, 2432), BF16),
            pltpu.VMEM((256, 2048), BF16),
            pltpu.VMEM((2, SLOTS, 384), F32),
            pltpu.VMEM((IRREPS, 2, 8, 384), F32),
            pltpu.VMEM((2, X, 2, 8, 384), F32),
            pltpu.VMEM((PLACES, SLOTS, 384), F32),
            pltpu.VMEM((2 * Z, 8, 384), F32),
            pltpu.VMEM((384, 384), F32),
            pltpu.VMEM((X, 2 * Z, 8, 128), F32),
            pltpu.VMEM((Z * PLACES, 8, 128), F32),
            pltpu.SemaphoreType.DMA((2,)),
            pltpu.SemaphoreType.DMA((PLACES,)),
            pltpu.SemaphoreType.DMA((6,)),
            pltpu.SemaphoreType.DMA((2 * Z,)),
            pltpu.SemaphoreType.DMA((Z * PLACES,)),
            pltpu.SemaphoreType.DMA,
            pltpu.SemaphoreType.DMA((2,)),
            pltpu.SemaphoreType.DMA,
            pltpu.SemaphoreType.DMA,
        ],
        compiler_params=pltpu.CompilerParams(
            collective_id=0, has_side_effects=True, vmem_limit_bytes=52 * 1024 * 1024
        ),
    )(
        amplitudes.T,
        integrals,
        row_sym[None, :],
        a_sym[:, None],
        w_sym[None, :],
        pad(bj_sym, BPAD, -1)[:, None],
        jnp.concatenate([a_code, a_code])[None, :],
        jnp.concatenate([bj_code, bj_code])[None, :],
        bj_code[:, None],
        rank_key[None, :],
        out_sym[None, :],
        out_shift[None, :],
        pad(bj_shift, BPAD, 1.0)[:, None],
    )
    return out.T


def solution(mesh):
    return jax.shard_map(
        local,
        mesh=mesh,
        in_specs=(P(None, "dist"), P("dist", "rep"), P(), P(), P(), P(), P()),
        out_specs=P("rep", "dist"),
        check_vma=False,
    )
```

```python
import jax
import jax.numpy as jnp
from jax import lax
from jax.experimental import pallas as pl
from jax.experimental.pallas import tpu as pltpu
from jax.sharding import PartitionSpec as P

MESH = pl.DeviceIdType.MESH
F32, BF16, I32 = jnp.float32, jnp.bfloat16, jnp.int32

O = 16
IRREPS = 8
Z, Y, X = 8, 4, 4
PLACES = 8
ROWS = 2816
COLS = 300
WIDE = 4800
HALF = 2400
BJ = 44
MY = 704
SLOTS = 40
QA = 88
APAD, BPAD = 304, 48
START = [(COLS * p) // O for p in range(PLACES)]


def halves(value):
    high = value.astype(BF16)
    return high, (value - high.astype(F32)).astype(BF16)


def matmul(left, right, dims):
    return lax.dot_general(left, right, (dims, ((), ())), preferred_element_type=F32)


NN = ((1,), (0,))
NT = ((1,), (1,))


def iota(shape, dim):
    return lax.broadcasted_iota(I32, shape, dim)


def exact(left, right, dims):
    return lax.dot_general(
        left, right, (dims, ((), ())), precision=lax.Precision.HIGHEST, preferred_element_type=F32
    )


def one_hot(mask):
    return mask.astype(F32)


def small(mask):
    return mask.astype(F32).astype(BF16)


def tiles(values, offset, count):
    size = values.shape[1]
    at = iota((count, size), 1) - offset
    parts = jnp.where((at >> 3) == iota((count, size), 0), values, 0.0)
    spread = ((iota((size, 128), 0) - offset) & 7) == (iota((size, 128), 1) >> 4)
    return parts, spread


def side_by_side(rows, first, count):
    return jnp.concatenate([rows[first + n : first + n + 1] for n in range(count)], axis=1)


def kernel(
    a_hbm,
    w_hbm,
    slab_ref,
    virtual_ref,
    occupied_ref,
    occupied_energy_ref,
    slab_energy_ref,
    out_ref,
    a_in,
    w_in,
    a_split,
    w_split,
    pick,
    a_msg,
    w_msg,
    w_mid,
    a_got,
    w_got,
    a_all,
    w_sym,
    o_msg,
    o_got,
    load_sem,
    a_send,
    x_send,
    w_send,
    o_send,
    a_recv,
    x_recv,
    w_recv,
    o_recv,
):
    d = lax.axis_index("dist")
    x = lax.axis_index("rep")
    z, place = d // PLACES, d % PLACES
    y, core = place // 2, place % 2
    load_a = pltpu.make_async_copy(a_hbm, a_in, load_sem.at[0])
    load_w = pltpu.make_async_copy(w_hbm, w_in, load_sem.at[1])
    load_w.start()
    load_a.start()

    barrier = pltpu.get_barrier_semaphore()

    def greet(dd, xx):
        pl.semaphore_signal(barrier, inc=1, device_id=(dd, xx), device_id_type=MESH)

    def greet_a(i, carry):
        greet(z * PLACES + (place + i) % PLACES, x)
        return carry

    def greet_o(i, carry):
        zs, cs, xs = (z + i // PLACES) % Z, (core + i) % 2, (x + (i % PLACES) // 2) % X
        greet(zs * PLACES + y * 2 + cs, xs)
        return carry

    lax.fori_loop(2 - core, PLACES - core, greet_a, 0)
    lax.fori_loop(1, Z * PLACES, greet_o, 0)

    slab = slab_ref[...].reshape(1, -1).astype(F32)
    virtual = virtual_ref[...].reshape(1, -1).astype(F32)
    occupied = occupied_ref[...].reshape(1, -1).astype(F32)
    occupied_energy = occupied_energy_ref[...].reshape(1, -1)
    slab_energy = slab_energy_ref[...].reshape(1, -1)
    n_slab, n_virtual = slab.shape[1], virtual.shape[1]
    slab_all = jnp.broadcast_to(slab, (128, n_slab)).astype(BF16)
    occ_all = jnp.broadcast_to(occupied, (128, O)).astype(BF16)

    repeat = iota((O, 128), 0) == (iota((O, 128), 1) & 15)
    occ_lane = matmul(occ_all[:16], small(repeat), NN)[:1].astype(I32)
    occ_energy_lane = exact(jnp.broadcast_to(occupied_energy, (8, O)), one_hot(repeat), NN)[:1]
    occ_col = matmul(small(iota((O, O), 0) == iota((O, O), 1)), occ_all, NT).astype(I32)
    earlier = (occ_col == occ_lane) & (iota((O, 128), 0) < (iota((O, 128), 1) & 15))
    rank = jnp.sum(one_hot(earlier), axis=0, keepdims=True)
    key = 2 * (iota((1, 128), 1) >> 4) + rank.astype(I32)

    parts, spread = tiles(slab, 0, 32)
    row_sym = matmul(parts.astype(BF16), small(spread), NN).astype(I32) ^ occ_lane
    parts, spread = tiles(slab, (MY // O) * x, 16)
    out_sym = matmul(parts.astype(BF16), small(spread), NN).astype(I32) ^ occ_lane
    parts, _ = tiles(slab_energy, (MY // O) * x, 8)
    out_shift = occ_energy_lane - exact(parts, one_hot(spread), NN)
    out_sym = side_by_side(out_sym, 0, 6)[:, :MY]
    out_shift = side_by_side(out_shift, 0, 6)[:, :MY]

    parts, spread = tiles(virtual, (WIDE // O) * x, 48)
    columns = matmul(parts.astype(BF16), small(spread), NN).astype(I32) ^ occ_lane
    for n in range(38):
        w_sym[:, pl.ds(n * 128, 128)] = columns[n : n + 1]

    first_c, inside = (COLS * d) // O, (COLS * d) % O
    near = small(iota((n_virtual, 128), 0) == first_c + iota((n_virtual, 128), 1))
    near = matmul(jnp.broadcast_to(virtual, (16, n_virtual)).astype(BF16), near, NN)
    near_all = jnp.broadcast_to(near[:1], (128, 128)).astype(BF16)
    at = inside + iota((APAD, 128), 0)
    v_col = matmul(small((at >> 4) == iota((APAD, 128), 1)), near_all, NT).astype(I32)
    at = inside + iota((APAD, O), 0)
    o_col = matmul(small((at & 15) == iota((APAD, O), 1)), occ_all, NT).astype(I32)
    a_col_sym = (v_col ^ o_col)[:COLS, :1]
    at = inside + iota((128, 384), 1)
    v_row = matmul(near_all[:16], small((at >> 4) == iota((128, 384), 0)), NN)[:1].astype(I32)
    at = inside + iota((O, 384), 1)
    pick_o = small((at & 15) == iota((O, 384), 0))
    o_row = matmul(occ_all[:16], pick_o, NN)[:1].astype(I32)
    rank_all = jnp.broadcast_to(rank[:, :O], (16, O)).astype(BF16)
    rank_row = matmul(rank_all, pick_o, NN)[:1].astype(I32)
    at = inside + iota((1, 384), 1)
    a_code = SLOTS * ((v_row ^ o_row) - 2 * x) + 2 * (at >> 4) + rank_row
    a_code = jnp.where(iota((1, 384), 1) < COLS, a_code, -1)[:, :APAD]

    at = BJ * d + iota((BPAD, n_slab), 0)
    pick_b = (at >> 4) == iota((BPAD, n_slab), 1)
    at = BJ * d + iota((BPAD, O), 0)
    pick_j = (at & 15) == iota((BPAD, O), 1)
    bj_col = matmul(small(pick_b), slab_all, NT).astype(I32) ^ matmul(
        small(pick_j), occ_all, NT
    ).astype(I32)
    bj_sym = jnp.where(iota((BPAD, 128), 0) < BJ, bj_col, -1)
    bj_shift = (
        exact(one_hot(pick_j), jnp.broadcast_to(occupied_energy, (128, O)), NT)
        - exact(one_hot(pick_b), jnp.broadcast_to(slab_energy, (128, n_slab)), NT)
    )[:, :1]
    at = BJ * d + iota((n_slab, 128), 1)
    b_row = matmul(slab_all[:16], small((at >> 4) == iota((n_slab, 128), 0)), NN)[:1]
    at = BJ * d + iota((O, 128), 1)
    j_row = matmul(occ_all[:16], small((at & 15) == iota((O, 128), 0)), NN)[:1]
    bj_row = jnp.where(iota((1, 128), 1) < BJ, b_row.astype(I32) ^ j_row.astype(I32), -1)
    same = bj_sym == bj_row
    shape = (BPAD, 128)
    slot_row = jnp.sum(one_hot(same & (iota(shape, 0) < iota(shape, 1))), axis=0, keepdims=True)
    slot_col = jnp.sum(one_hot(same & (iota(shape, 1) < iota(shape, 0))), axis=1, keepdims=True)
    bj_code = jnp.where(bj_row < 0, -1, 8 * bj_row + slot_row.astype(I32))[:, :BPAD]
    bj_sym = bj_sym[:, :1]
    bj_code_col = jnp.where(bj_sym < 0, -1, 8 * bj_sym + slot_col.astype(I32))

    for n in range(16):
        pick[:, pl.ds(n * 128, 128)] = small(key + 16 * n == iota((256, 128), 0))
    for n in range(4):
        o_msg[n] = jnp.zeros((2 * Z, 8, 128), F32)
        w_split[pl.ds(n * BPAD + 32, 16)] = jnp.zeros((16, 2432), BF16)
    for n in range(2):
        a_split[pl.ds(n * APAD + 288, 16)] = jnp.zeros((16, ROWS), BF16)

    load_w.wait()
    for half in range(2):
        cols = pl.ds(half * HALF, HALF)
        kept = jnp.where(bj_sym[:BJ] == w_sym[:, cols], w_in[:, cols], 0.0)
        high, low = halves(kept)
        w_split[pl.ds(half * 2 * BPAD, BJ), pl.ds(0, HALF)] = high
        w_split[pl.ds((half * 2 + 1) * BPAD, BJ), pl.ds(0, HALF)] = low
    w_main = matmul(w_split[:, pl.ds(0, 2048)], pick[...], NT)
    w_rest = matmul(
        w_split[:, pl.ds(2048, HALF - 2048)], pick[pl.ds(0, 128), pl.ds(0, HALF - 2048)], NT
    )
    group = small(iota((IRREPS * 8, BPAD), 0) == bj_code)
    for half in range(2):
        rows = [slice((2 * half + n) * BPAD, (2 * half + n + 1) * BPAD) for n in range(2)]
        main = sum(matmul(group, w_main[r].astype(BF16), NN) for r in rows)
        rest = sum(matmul(group, w_rest[r].astype(BF16), NN) for r in rows)
        w_msg[:, half, :, pl.ds(0, 256)] = main.reshape(IRREPS, 8, 256)
        w_msg[:, half, :, pl.ds(256, 128)] = rest.reshape(IRREPS, 8, 128)

    pl.semaphore_wait(barrier, 6 + Z * PLACES - 1)

    def x_copy(i):
        cs, xs = (core + i // 3) % 2, (x + 1 + i % 3) % X
        return pltpu.make_async_remote_copy(
            src_ref=w_msg.at[2 * xs + cs],
            dst_ref=w_mid.at[cs, x],
            send_sem=x_send.at[i],
            recv_sem=x_recv.at[cs],
            device_id=(d, xs),
            device_id_type=MESH,
        )

    def send_x(i, carry):
        x_copy(i).start()
        return carry

    lax.fori_loop(0, 6, send_x, 0)
    for cs in range(2):
        pltpu.make_async_copy(w_msg.at[2 * x + cs], w_mid.at[cs, x], x_recv.at[cs]).start()

    load_a.wait()
    for n in range(11):
        cols = pl.ds(n * 256, 256)
        kept = jnp.where(
            a_col_sym == side_by_side(row_sym, 2 * n, 2), a_in[:, cols], 0.0
        )
        high, low = halves(kept)
        a_split[pl.ds(0, COLS), cols] = high
        a_split[pl.ds(APAD, COLS), cols] = low
    a_main = matmul(a_split[:, pl.ds(0, 2048)], pick[...], NT)
    a_rest = matmul(
        a_split[:, pl.ds(2048, ROWS - 2048)], pick[pl.ds(0, 128), pl.ds(0, ROWS - 2048)], NT
    )
    place_rows = small(iota((2 * SLOTS, APAD), 0) == a_code)
    rows = [slice(n * APAD, (n + 1) * APAD) for n in range(2)]
    main = sum(matmul(place_rows, a_main[r].astype(BF16), NN) for r in rows)
    rest = sum(matmul(place_rows, a_rest[r].astype(BF16), NN) for r in rows)
    a_msg[:, :, pl.ds(0, 256)] = main.reshape(2, SLOTS, 256)
    a_msg[:, :, pl.ds(256, 128)] = rest.reshape(2, SLOTS, 128)

    def a_copy(i):
        to = (place + i) % PLACES
        return pltpu.make_async_remote_copy(
            src_ref=a_msg.at[to % 2],
            dst_ref=a_got.at[place],
            send_sem=a_send.at[i],
            recv_sem=a_recv,
            device_id=(z * PLACES + to, x),
            device_id_type=MESH,
        )

    def send_a(i, carry):
        a_copy(i).start()
        return carry

    lax.fori_loop(1, PLACES, send_a, 0)
    pltpu.make_async_copy(a_msg.at[core], a_got.at[place], a_recv).start()

    slot_w = z * 2 + core

    def w_copy(i):
        cs, zs = (core + i // Z) % 2, (z + i) % Z
        return pltpu.make_async_remote_copy(
            src_ref=w_mid.at[cs, zs // 2, zs % 2],
            dst_ref=w_got.at[slot_w],
            send_sem=w_send.at[i],
            recv_sem=w_recv,
            device_id=(zs * PLACES + y * 2 + cs, x),
            device_id_type=MESH,
        )

    def send_w(i, carry):
        w_copy(i).start()
        return carry

    first, second = w_mid.at[core], w_mid.at[1 - core]
    pltpu.make_async_copy(first, first, x_recv.at[core]).wait()
    pltpu.make_async_copy(first.at[z // 2, z % 2], w_got.at[slot_w], w_recv).start()
    lax.fori_loop(1, Z, send_w, 0)
    pltpu.make_async_copy(second, second, x_recv.at[1 - core]).wait()
    lax.fori_loop(Z, 2 * Z, send_w, 0)

    a_all[...] = jnp.zeros(a_all.shape, F32)
    pltpu.make_async_copy(a_got, a_got, a_recv).wait()
    for p in range(PLACES):
        first = 2 * START[p]
        a_all[pl.ds(first, SLOTS), :] += a_got[p]
    pltpu.make_async_copy(w_got, w_got, w_recv).wait()
    w_high, w_low = halves(w_got[...].reshape(2 * Z * 8, 384))
    a_high, a_low = halves(a_all[...])
    product = matmul(w_high, a_low, NN) + matmul(w_low, a_high, NN)
    product = product + matmul(w_high, a_high, NN)
    for part in range(X):
        o_msg[part, :, :, pl.ds(0, QA)] = product[:, part * QA : (part + 1) * QA].reshape(
            2 * Z, 8, QA
        )

    def o_copy(i):
        zs, cs, part = (z + i // PLACES) % Z, (core + i) % 2, (x + (i % PLACES) // 2) % X
        return pltpu.make_async_remote_copy(
            src_ref=o_msg.at[part, zs * 2 + cs],
            dst_ref=o_got.at[z * PLACES + 2 * x + core],
            send_sem=o_send.at[i],
            recv_sem=o_recv,
            device_id=(zs * PLACES + y * 2 + cs, part),
            device_id_type=MESH,
        )

    def send_o(i, carry):
        o_copy(i).start()
        return carry

    lax.fori_loop(1, Z * PLACES, send_o, 0)
    pltpu.make_async_copy(
        o_msg.at[x, slot_w], o_got.at[z * PLACES + 2 * x + core], o_recv
    ).start()

    spread = small((iota((BPAD, 128), 1) & 63) == bj_code_col)
    pltpu.make_async_copy(o_got, o_got, o_recv).wait()
    total = o_got[pl.ds(0, PLACES)]
    for zs in range(1, Z):
        total = total + o_got[pl.ds(zs * PLACES, PLACES)]
    high, low = halves(total.reshape(IRREPS * 8, 128))
    mine = matmul(spread, jnp.concatenate([high, low], axis=0), NN)
    high, low = halves(mine)
    widen = pick[pl.ds(0, 128), pl.ds(0, MY)]
    cycle = matmul(high, widen, NN) + matmul(low, widen, NN)
    value = jnp.where(bj_sym == out_sym, cycle, 0.0) / (out_shift + bj_shift)
    out_ref[...] = value[:BJ]

    def done_x(i, carry):
        x_copy(i).wait_send()
        return carry

    def done_w(i, carry):
        w_copy(i).wait_send()
        return carry

    def done_a(i, carry):
        a_copy(i).wait_send()
        return carry

    def done_o(i, carry):
        o_copy(i).wait_send()
        return carry

    lax.fori_loop(0, 6, done_x, 0)
    lax.fori_loop(1, 2 * Z, done_w, 0)
    lax.fori_loop(1, PLACES, done_a, 0)
    lax.fori_loop(1, Z * PLACES, done_o, 0)


def local(
    amplitudes, integrals, slab_irrep, virtual_irrep, occupied_irrep, occupied_energy, slab_energy
):
    vmem = pl.BlockSpec(memory_space=pltpu.VMEM)
    hbm = pl.BlockSpec(memory_space=pl.ANY)
    out = pl.pallas_call(
        kernel,
        out_shape=jax.ShapeDtypeStruct((BJ, MY), F32),
        in_specs=[hbm, hbm] + [vmem] * 5,
        out_specs=vmem,
        scratch_shapes=[
            pltpu.VMEM((COLS, ROWS), F32),
            pltpu.VMEM((BJ, WIDE), F32),
            pltpu.VMEM((2 * APAD, ROWS), BF16),
            pltpu.VMEM((4 * BPAD, 2432), BF16),
            pltpu.VMEM((256, 2048), BF16),
            pltpu.VMEM((2, SLOTS, 384), F32),
            pltpu.VMEM((IRREPS, 2, 8, 384), F32),
            pltpu.VMEM((2, X, 2, 8, 384), F32),
            pltpu.VMEM((PLACES, SLOTS, 384), F32),
            pltpu.VMEM((2 * Z, 8, 384), F32),
            pltpu.VMEM((384, 384), F32),
            pltpu.VMEM((1, 38 * 128), I32),
            pltpu.VMEM((X, 2 * Z, 8, 128), F32),
            pltpu.VMEM((Z * PLACES, 8, 128), F32),
            pltpu.SemaphoreType.DMA((2,)),
            pltpu.SemaphoreType.DMA((PLACES,)),
            pltpu.SemaphoreType.DMA((6,)),
            pltpu.SemaphoreType.DMA((2 * Z,)),
            pltpu.SemaphoreType.DMA((Z * PLACES,)),
            pltpu.SemaphoreType.DMA,
            pltpu.SemaphoreType.DMA((2,)),
            pltpu.SemaphoreType.DMA,
            pltpu.SemaphoreType.DMA,
        ],
        compiler_params=pltpu.CompilerParams(
            collective_id=0, has_side_effects=True, vmem_limit_bytes=52 * 1024 * 1024
        ),
    )(
        amplitudes.T,
        integrals,
        slab_irrep,
        virtual_irrep,
        occupied_irrep,
        occupied_energy,
        slab_energy,
    )
    return out.T


def solution(mesh):
    return jax.shard_map(
        local,
        mesh=mesh,
        in_specs=(P(None, "dist"), P("dist", "rep"), P(), P(), P(), P(), P()),
        out_specs=P("rep", "dist"),
        check_vma=False,
    )
```

```python
import jax
import jax.numpy as jnp
from jax import lax
from jax.experimental import pallas as pl
from jax.experimental.pallas import tpu as pltpu
from jax.sharding import PartitionSpec as P

MESH = pl.DeviceIdType.MESH
F32, BF16, I32 = jnp.float32, jnp.bfloat16, jnp.int32

O = 16
IRREPS = 8
Z, Y, X = 8, 4, 4
PLACES = 8
ROWS = 2816
COLS = 300
WIDE = 4800
HALF = 2400
BJ = 44
MY = 704
SLOTS = 40
QA = 88
APAD, BPAD = 304, 48
START = [(COLS * p) // O for p in range(PLACES)]


def halves(value):
    high = value.astype(BF16)
    return high, (value - high.astype(F32)).astype(BF16)


def matmul(left, right, dims):
    return lax.dot_general(left, right, (dims, ((), ())), preferred_element_type=F32)


NN = ((1,), (0,))
NT = ((1,), (1,))


def iota(shape, dim):
    return lax.broadcasted_iota(I32, shape, dim)


def exact(left, right, dims):
    return lax.dot_general(
        left, right, (dims, ((), ())), precision=lax.Precision.HIGHEST, preferred_element_type=F32
    )


def one_hot(mask):
    return mask.astype(F32)


def small(mask):
    return mask.astype(F32).astype(BF16)


def tiles(values, offset, count):
    size = values.shape[1]
    at = iota((count, size), 1) - offset
    parts = jnp.where((at >> 3) == iota((count, size), 0), values, 0.0)
    spread = ((iota((size, 128), 0) - offset) & 7) == (iota((size, 128), 1) >> 4)
    return parts, spread


def side_by_side(rows, first, count):
    return jnp.concatenate([rows[first + n : first + n + 1] for n in range(count)], axis=1)


def kernel(
    a_hbm,
    w_hbm,
    slab_hbm,
    virtual_hbm,
    occupied_hbm,
    occupied_energy_hbm,
    slab_energy_hbm,
    out_ref,
    slab_ref,
    virtual_ref,
    occupied_ref,
    occupied_energy_ref,
    slab_energy_ref,
    a_in,
    w_in,
    a_split,
    w_split,
    pick,
    a_msg,
    w_msg,
    w_mid,
    a_got,
    w_got,
    a_all,
    w_sym,
    o_msg,
    o_got,
    load_sem,
    a_send,
    x_send,
    w_send,
    o_send,
    a_recv,
    x_recv,
    w_recv,
    o_recv,
):
    d = lax.axis_index("dist")
    x = lax.axis_index("rep")
    z, place = d // PLACES, d % PLACES
    y, core = place // 2, place % 2
    load_a = pltpu.make_async_copy(a_hbm, a_in, load_sem.at[0])
    load_w = pltpu.make_async_copy(w_hbm, w_in, load_sem.at[1])
    loads = [
        pltpu.make_async_copy(source, target, load_sem.at[2 + n])
        for n, (source, target) in enumerate(
            [
                (occupied_hbm, occupied_ref),
                (slab_hbm, slab_ref),
                (virtual_hbm, virtual_ref),
                (occupied_energy_hbm, occupied_energy_ref),
                (slab_energy_hbm, slab_energy_ref),
            ]
        )
    ]
    for load in loads:
        load.start()
    load_w.start()
    load_a.start()

    barrier = pltpu.get_barrier_semaphore()

    def greet(dd, xx):
        pl.semaphore_signal(barrier, inc=1, device_id=(dd, xx), device_id_type=MESH)

    def greet_a(i, carry):
        greet(z * PLACES + (place + i) % PLACES, x)
        return carry

    def greet_o(i, carry):
        zs, cs, xs = (z + i // PLACES) % Z, (core + i) % 2, (x + (i % PLACES) // 2) % X
        greet(zs * PLACES + y * 2 + cs, xs)
        return carry

    lax.fori_loop(2 - core, PLACES - core, greet_a, 0)
    lax.fori_loop(1, Z * PLACES, greet_o, 0)

    for load in loads:
        load.wait()
    slab = slab_ref[...].reshape(1, -1).astype(F32)
    virtual = virtual_ref[...].reshape(1, -1).astype(F32)
    occupied = occupied_ref[...].reshape(1, -1).astype(F32)
    occupied_energy = occupied_energy_ref[...].reshape(1, -1)
    slab_energy = slab_energy_ref[...].reshape(1, -1)
    n_slab, n_virtual = slab.shape[1], virtual.shape[1]
    slab_all = jnp.broadcast_to(slab, (128, n_slab)).astype(BF16)
    occ_all = jnp.broadcast_to(occupied, (128, O)).astype(BF16)

    repeat = iota((O, 128), 0) == (iota((O, 128), 1) & 15)
    occ_lane = matmul(occ_all[:16], small(repeat), NN)[:1].astype(I32)
    occ_energy_lane = exact(jnp.broadcast_to(occupied_energy, (8, O)), one_hot(repeat), NN)[:1]
    occ_col = matmul(small(iota((O, O), 0) == iota((O, O), 1)), occ_all, NT).astype(I32)
    earlier = (occ_col == occ_lane) & (iota((O, 128), 0) < (iota((O, 128), 1) & 15))
    rank = jnp.sum(one_hot(earlier), axis=0, keepdims=True)
    key = 2 * (iota((1, 128), 1) >> 4) + rank.astype(I32)

    parts, spread = tiles(slab, 0, 32)
    row_sym = matmul(parts.astype(BF16), small(spread), NN).astype(I32) ^ occ_lane
    parts, spread = tiles(slab, (MY // O) * x, 16)
    out_sym = matmul(parts.astype(BF16), small(spread), NN).astype(I32) ^ occ_lane
    parts, _ = tiles(slab_energy, (MY // O) * x, 8)
    out_shift = occ_energy_lane - exact(parts, one_hot(spread), NN)
    out_sym = side_by_side(out_sym, 0, 6)[:, :MY]
    out_shift = side_by_side(out_shift, 0, 6)[:, :MY]

    parts, spread = tiles(virtual, (WIDE // O) * x, 48)
    columns = matmul(parts.astype(BF16), small(spread), NN).astype(I32) ^ occ_lane
    for n in range(38):
        w_sym[:, pl.ds(n * 128, 128)] = columns[n : n + 1]

    first_c, inside = (COLS * d) // O, (COLS * d) % O
    near = small(iota((n_virtual, 128), 0) == first_c + iota((n_virtual, 128), 1))
    near = matmul(jnp.broadcast_to(virtual, (16, n_virtual)).astype(BF16), near, NN)
    near_all = jnp.broadcast_to(near[:1], (128, 128)).astype(BF16)
    at = inside + iota((APAD, 128), 0)
    v_col = matmul(small((at >> 4) == iota((APAD, 128), 1)), near_all, NT).astype(I32)
    at = inside + iota((APAD, O), 0)
    o_col = matmul(small((at & 15) == iota((APAD, O), 1)), occ_all, NT).astype(I32)
    a_col_sym = (v_col ^ o_col)[:COLS, :1]
    at = inside + iota((128, 384), 1)
    v_row = matmul(near_all[:16], small((at >> 4) == iota((128, 384), 0)), NN)[:1].astype(I32)
    at = inside + iota((O, 384), 1)
    pick_o = small((at & 15) == iota((O, 384), 0))
    o_row = matmul(occ_all[:16], pick_o, NN)[:1].astype(I32)
    rank_all = jnp.broadcast_to(rank[:, :O], (16, O)).astype(BF16)
    rank_row = matmul(rank_all, pick_o, NN)[:1].astype(I32)
    at = inside + iota((1, 384), 1)
    a_code = SLOTS * ((v_row ^ o_row) - 2 * x) + 2 * (at >> 4) + rank_row
    a_code = jnp.where(iota((1, 384), 1) < COLS, a_code, -1)[:, :APAD]

    at = BJ * d + iota((BPAD, n_slab), 0)
    pick_b = (at >> 4) == iota((BPAD, n_slab), 1)
    at = BJ * d + iota((BPAD, O), 0)
    pick_j = (at & 15) == iota((BPAD, O), 1)
    bj_col = matmul(small(pick_b), slab_all, NT).astype(I32) ^ matmul(
        small(pick_j), occ_all, NT
    ).astype(I32)
    bj_sym = jnp.where(iota((BPAD, 128), 0) < BJ, bj_col, -1)
    bj_shift = (
        exact(one_hot(pick_j), jnp.broadcast_to(occupied_energy, (128, O)), NT)
        - exact(one_hot(pick_b), jnp.broadcast_to(slab_energy, (128, n_slab)), NT)
    )[:, :1]
    at = BJ * d + iota((n_slab, 128), 1)
    b_row = matmul(slab_all[:16], small((at >> 4) == iota((n_slab, 128), 0)), NN)[:1]
    at = BJ * d + iota((O, 128), 1)
    j_row = matmul(occ_all[:16], small((at & 15) == iota((O, 128), 0)), NN)[:1]
    bj_row = jnp.where(iota((1, 128), 1) < BJ, b_row.astype(I32) ^ j_row.astype(I32), -1)
    same = bj_sym == bj_row
    shape = (BPAD, 128)
    slot_row = jnp.sum(one_hot(same & (iota(shape, 0) < iota(shape, 1))), axis=0, keepdims=True)
    slot_col = jnp.sum(one_hot(same & (iota(shape, 1) < iota(shape, 0))), axis=1, keepdims=True)
    bj_code = jnp.where(bj_row < 0, -1, 8 * bj_row + slot_row.astype(I32))[:, :BPAD]
    bj_sym = bj_sym[:, :1]
    bj_code_col = jnp.where(bj_sym < 0, -1, 8 * bj_sym + slot_col.astype(I32))

    for n in range(16):
        pick[:, pl.ds(n * 128, 128)] = small(key + 16 * n == iota((256, 128), 0))
    for n in range(4):
        o_msg[n] = jnp.zeros((2 * Z, 8, 128), F32)
        w_split[pl.ds(n * BPAD + 32, 16)] = jnp.zeros((16, 2432), BF16)
    for n in range(2):
        a_split[pl.ds(n * APAD + 288, 16)] = jnp.zeros((16, ROWS), BF16)

    load_w.wait()
    for half in range(2):
        cols = pl.ds(half * HALF, HALF)
        kept = jnp.where(bj_sym[:BJ] == w_sym[:, cols], w_in[:, cols], 0.0)
        high, low = halves(kept)
        w_split[pl.ds(half * 2 * BPAD, BJ), pl.ds(0, HALF)] = high
        w_split[pl.ds((half * 2 + 1) * BPAD, BJ), pl.ds(0, HALF)] = low
    w_main = matmul(w_split[:, pl.ds(0, 2048)], pick[...], NT)
    w_rest = matmul(
        w_split[:, pl.ds(2048, HALF - 2048)], pick[pl.ds(0, 128), pl.ds(0, HALF - 2048)], NT
    )
    group = small(iota((IRREPS * 8, BPAD), 0) == bj_code)
    for half in range(2):
        rows = [slice((2 * half + n) * BPAD, (2 * half + n + 1) * BPAD) for n in range(2)]
        main = sum(matmul(group, w_main[r].astype(BF16), NN) for r in rows)
        rest = sum(matmul(group, w_rest[r].astype(BF16), NN) for r in rows)
        w_msg[:, half, :, pl.ds(0, 256)] = main.reshape(IRREPS, 8, 256)
        w_msg[:, half, :, pl.ds(256, 128)] = rest.reshape(IRREPS, 8, 128)

    pl.semaphore_wait(barrier, 6 + Z * PLACES - 1)

    def x_copy(i):
        cs, xs = (core + i // 3) % 2, (x + 1 + i % 3) % X
        return pltpu.make_async_remote_copy(
            src_ref=w_msg.at[2 * xs + cs],
            dst_ref=w_mid.at[cs, x],
            send_sem=x_send.at[i],
            recv_sem=x_recv.at[cs],
            device_id=(d, xs),
            device_id_type=MESH,
        )

    def send_x(i, carry):
        x_copy(i).start()
        return carry

    lax.fori_loop(0, 6, send_x, 0)
    for cs in range(2):
        pltpu.make_async_copy(w_msg.at[2 * x + cs], w_mid.at[cs, x], x_recv.at[cs]).start()

    load_a.wait()
    for n in range(11):
        cols = pl.ds(n * 256, 256)
        kept = jnp.where(
            a_col_sym == side_by_side(row_sym, 2 * n, 2), a_in[:, cols], 0.0
        )
        high, low = halves(kept)
        a_split[pl.ds(0, COLS), cols] = high
        a_split[pl.ds(APAD, COLS), cols] = low
    a_main = matmul(a_split[:, pl.ds(0, 2048)], pick[...], NT)
    a_rest = matmul(
        a_split[:, pl.ds(2048, ROWS - 2048)], pick[pl.ds(0, 128), pl.ds(0, ROWS - 2048)], NT
    )
    place_rows = small(iota((2 * SLOTS, APAD), 0) == a_code)
    rows = [slice(n * APAD, (n + 1) * APAD) for n in range(2)]
    main = sum(matmul(place_rows, a_main[r].astype(BF16), NN) for r in rows)
    rest = sum(matmul(place_rows, a_rest[r].astype(BF16), NN) for r in rows)
    a_msg[:, :, pl.ds(0, 256)] = main.reshape(2, SLOTS, 256)
    a_msg[:, :, pl.ds(256, 128)] = rest.reshape(2, SLOTS, 128)

    def a_copy(i):
        to = (place + i) % PLACES
        return pltpu.make_async_remote_copy(
            src_ref=a_msg.at[to % 2],
            dst_ref=a_got.at[place],
            send_sem=a_send.at[i],
            recv_sem=a_recv,
            device_id=(z * PLACES + to, x),
            device_id_type=MESH,
        )

    def send_a(i, carry):
        a_copy(i).start()
        return carry

    lax.fori_loop(1, PLACES, send_a, 0)
    pltpu.make_async_copy(a_msg.at[core], a_got.at[place], a_recv).start()

    slot_w = z * 2 + core

    def w_copy(i):
        cs, zs = (core + i // Z) % 2, (z + i) % Z
        return pltpu.make_async_remote_copy(
            src_ref=w_mid.at[cs, zs // 2, zs % 2],
            dst_ref=w_got.at[slot_w],
            send_sem=w_send.at[i],
            recv_sem=w_recv,
            device_id=(zs * PLACES + y * 2 + cs, x),
            device_id_type=MESH,
        )

    def send_w(i, carry):
        w_copy(i).start()
        return carry

    first, second = w_mid.at[core], w_mid.at[1 - core]
    pltpu.make_async_copy(first, first, x_recv.at[core]).wait()
    pltpu.make_async_copy(first.at[z // 2, z % 2], w_got.at[slot_w], w_recv).start()
    lax.fori_loop(1, Z, send_w, 0)
    pltpu.make_async_copy(second, second, x_recv.at[1 - core]).wait()
    lax.fori_loop(Z, 2 * Z, send_w, 0)

    a_all[...] = jnp.zeros(a_all.shape, F32)
    pltpu.make_async_copy(a_got, a_got, a_recv).wait()
    for p in range(PLACES):
        first = 2 * START[p]
        a_all[pl.ds(first, SLOTS), :] += a_got[p]
    pltpu.make_async_copy(w_got, w_got, w_recv).wait()
    w_high, w_low = halves(w_got[...].reshape(2 * Z * 8, 384))
    a_high, a_low = halves(a_all[...])
    product = matmul(w_high, a_low, NN) + matmul(w_low, a_high, NN)
    product = product + matmul(w_high, a_high, NN)
    for part in range(X):
        o_msg[part, :, :, pl.ds(0, QA)] = product[:, part * QA : (part + 1) * QA].reshape(
            2 * Z, 8, QA
        )

    def o_copy(i):
        zs, cs, part = (z + i // PLACES) % Z, (core + i) % 2, (x + (i % PLACES) // 2) % X
        return pltpu.make_async_remote_copy(
            src_ref=o_msg.at[part, zs * 2 + cs],
            dst_ref=o_got.at[z * PLACES + 2 * x + core],
            send_sem=o_send.at[i],
            recv_sem=o_recv,
            device_id=(zs * PLACES + y * 2 + cs, part),
            device_id_type=MESH,
        )

    def send_o(i, carry):
        o_copy(i).start()
        return carry

    lax.fori_loop(1, Z * PLACES, send_o, 0)
    pltpu.make_async_copy(
        o_msg.at[x, slot_w], o_got.at[z * PLACES + 2 * x + core], o_recv
    ).start()

    spread = small((iota((BPAD, 128), 1) & 63) == bj_code_col)
    pltpu.make_async_copy(o_got, o_got, o_recv).wait()
    total = o_got[pl.ds(0, PLACES)]
    for zs in range(1, Z):
        total = total + o_got[pl.ds(zs * PLACES, PLACES)]
    high, low = halves(total.reshape(IRREPS * 8, 128))
    mine = matmul(spread, jnp.concatenate([high, low], axis=0), NN)
    high, low = halves(mine)
    widen = pick[pl.ds(0, 128), pl.ds(0, MY)]
    cycle = matmul(high, widen, NN) + matmul(low, widen, NN)
    value = jnp.where(bj_sym == out_sym, cycle, 0.0) / (out_shift + bj_shift)
    out_ref[...] = value[:BJ]

    def done_x(i, carry):
        x_copy(i).wait_send()
        return carry

    def done_w(i, carry):
        w_copy(i).wait_send()
        return carry

    def done_a(i, carry):
        a_copy(i).wait_send()
        return carry

    def done_o(i, carry):
        o_copy(i).wait_send()
        return carry

    lax.fori_loop(0, 6, done_x, 0)
    lax.fori_loop(1, 2 * Z, done_w, 0)
    lax.fori_loop(1, PLACES, done_a, 0)
    lax.fori_loop(1, Z * PLACES, done_o, 0)


def local(
    amplitudes, integrals, slab_irrep, virtual_irrep, occupied_irrep, occupied_energy, slab_energy
):
    vmem = pl.BlockSpec(memory_space=pltpu.VMEM)
    hbm = pl.BlockSpec(memory_space=pltpu.HBM)
    out = pl.pallas_call(
        kernel,
        out_shape=jax.ShapeDtypeStruct((BJ, MY), F32),
        in_specs=[hbm] * 7,
        out_specs=vmem,
        scratch_shapes=[
            pltpu.VMEM(slab_irrep.shape, I32),
            pltpu.VMEM(virtual_irrep.shape, I32),
            pltpu.VMEM(occupied_irrep.shape, I32),
            pltpu.VMEM(occupied_energy.shape, F32),
            pltpu.VMEM(slab_energy.shape, F32),
            pltpu.VMEM((COLS, ROWS), F32),
            pltpu.VMEM((BJ, WIDE), F32),
            pltpu.VMEM((2 * APAD, ROWS), BF16),
            pltpu.VMEM((4 * BPAD, 2432), BF16),
            pltpu.VMEM((256, 2048), BF16),
            pltpu.VMEM((2, SLOTS, 384), F32),
            pltpu.VMEM((IRREPS, 2, 8, 384), F32),
            pltpu.VMEM((2, X, 2, 8, 384), F32),
            pltpu.VMEM((PLACES, SLOTS, 384), F32),
            pltpu.VMEM((2 * Z, 8, 384), F32),
            pltpu.VMEM((384, 384), F32),
            pltpu.VMEM((1, 38 * 128), I32),
            pltpu.VMEM((X, 2 * Z, 8, 128), F32),
            pltpu.VMEM((Z * PLACES, 8, 128), F32),
            pltpu.SemaphoreType.DMA((7,)),
            pltpu.SemaphoreType.DMA((PLACES,)),
            pltpu.SemaphoreType.DMA((6,)),
            pltpu.SemaphoreType.DMA((2 * Z,)),
            pltpu.SemaphoreType.DMA((Z * PLACES,)),
            pltpu.SemaphoreType.DMA,
            pltpu.SemaphoreType.DMA((2,)),
            pltpu.SemaphoreType.DMA,
            pltpu.SemaphoreType.DMA,
        ],
        compiler_params=pltpu.CompilerParams(
            collective_id=0, has_side_effects=True, vmem_limit_bytes=58 << 20
        ),
    )(
        amplitudes.T,
        integrals,
        slab_irrep,
        virtual_irrep,
        occupied_irrep,
        occupied_energy,
        slab_energy,
    )
    return out.T


def solution(mesh):
    return jax.shard_map(
        local,
        mesh=mesh,
        in_specs=(P(None, "dist"), P("dist", "rep"), P(), P(), P(), P(), P()),
        out_specs=P("rep", "dist"),
        check_vma=False,
    )
```

```python
import jax
import jax.numpy as jnp
from jax import lax
from jax.experimental import pallas as pl
from jax.experimental.pallas import tpu as pltpu
from jax.sharding import PartitionSpec as P

MESH = pl.DeviceIdType.MESH
F32, BF16, I32 = jnp.float32, jnp.bfloat16, jnp.int32

O = 16
IRREPS = 8
Z, Y, X = 8, 4, 4
PLACES = 8
ROWS = 2816
COLS = 300
WIDE = 4800
HALF = 2400
BJ = 44
MY = 704
SLOTS = 40
QA = 88
APAD, BPAD = 304, 48
START = [(COLS * p) // O for p in range(PLACES)]


def halves(value):
    high = value.astype(BF16)
    return high, (value - high.astype(F32)).astype(BF16)


def matmul(left, right, dims):
    return lax.dot_general(left, right, (dims, ((), ())), preferred_element_type=F32)


NN = ((1,), (0,))
NT = ((1,), (1,))


def iota(shape, dim):
    return lax.broadcasted_iota(I32, shape, dim)


def exact(left, right, dims):
    return lax.dot_general(
        left, right, (dims, ((), ())), precision=lax.Precision.HIGHEST, preferred_element_type=F32
    )


def one_hot(mask):
    return mask.astype(F32)


def small(mask):
    return mask.astype(F32).astype(BF16)


def tiles(values, offset, count):
    size = values.shape[1]
    at = iota((count, size), 1) - offset
    parts = jnp.where((at >> 3) == iota((count, size), 0), values, 0.0)
    spread = ((iota((size, 128), 0) - offset) & 7) == (iota((size, 128), 1) >> 4)
    return parts, spread


FAR_FIRST = (4, 5, 3, 6, 2, 7, 1, 0)


def side_by_side(rows, first, count):
    return jnp.concatenate([rows[first + n : first + n + 1] for n in range(count)], axis=1)


def kernel(
    a_hbm,
    w_hbm,
    slab_hbm,
    virtual_hbm,
    occupied_hbm,
    occupied_energy_hbm,
    slab_energy_hbm,
    out_ref,
    slab_ref,
    virtual_ref,
    occupied_ref,
    occupied_energy_ref,
    slab_energy_ref,
    a_in,
    w_in,
    a_split,
    w_split,
    pick,
    a_msg,
    w_msg,
    w_mid,
    a_got,
    w_got,
    a_all,
    w_sym,
    o_msg,
    o_got,
    load_sem,
    a_send,
    x_send,
    w_send,
    o_send,
    a_recv,
    x_recv,
    w_recv,
    o_recv,
):
    d = lax.axis_index("dist")
    x = lax.axis_index("rep")
    z, place = lax.div(d, PLACES), lax.rem(d, PLACES)
    y, core = lax.div(place, 2), lax.rem(place, 2)
    z_at = [lax.rem(z + n, Z) for n in range(Z)]
    y_at = [lax.rem(y + n, Y) for n in range(Y)]
    x_at = [lax.rem(x + n, X) for n in range(X)]
    core_at = [core, 1 - core]
    here = y * 2
    load_a = pltpu.make_async_copy(a_hbm, a_in, load_sem.at[0])
    load_w = pltpu.make_async_copy(w_hbm, w_in, load_sem.at[1])
    loads = [
        pltpu.make_async_copy(source, target, load_sem.at[2 + n])
        for n, (source, target) in enumerate(
            [
                (occupied_hbm, occupied_ref),
                (slab_hbm, slab_ref),
                (virtual_hbm, virtual_ref),
                (occupied_energy_hbm, occupied_energy_ref),
                (slab_energy_hbm, slab_energy_ref),
            ]
        )
    ]
    for load in loads:
        load.start()
    load_w.start()
    load_a.start()

    barrier = pltpu.get_barrier_semaphore()

    def greet(dd, xx):
        pl.semaphore_signal(barrier, inc=1, device_id=(dd, xx), device_id_type=MESH)

    for n in FAR_FIRST:
        for m in range(X):
            for j in range(2):
                if n or m or j:
                    greet(z_at[n] * PLACES + here + core_at[j], x_at[m])
    for m in range(1, Y):
        for j in range(2):
            greet(z * PLACES + y_at[m] * 2 + core_at[j], x)

    for load in loads:
        load.wait()
    slab = slab_ref[...].reshape(1, -1).astype(F32)
    virtual = virtual_ref[...].reshape(1, -1).astype(F32)
    occupied = occupied_ref[...].reshape(1, -1).astype(F32)
    occupied_energy = occupied_energy_ref[...].reshape(1, -1)
    slab_energy = slab_energy_ref[...].reshape(1, -1)
    n_slab, n_virtual = slab.shape[1], virtual.shape[1]
    slab_all = jnp.broadcast_to(slab, (128, n_slab)).astype(BF16)
    occ_all = jnp.broadcast_to(occupied, (128, O)).astype(BF16)

    repeat = iota((O, 128), 0) == (iota((O, 128), 1) & 15)
    occ_lane = matmul(occ_all[:16], small(repeat), NN)[:1].astype(I32)
    occ_energy_lane = exact(jnp.broadcast_to(occupied_energy, (8, O)), one_hot(repeat), NN)[:1]
    occ_col = matmul(small(iota((O, O), 0) == iota((O, O), 1)), occ_all, NT).astype(I32)
    earlier = (occ_col == occ_lane) & (iota((O, 128), 0) < (iota((O, 128), 1) & 15))
    rank = jnp.sum(one_hot(earlier), axis=0, keepdims=True)
    key = 2 * (iota((1, 128), 1) >> 4) + rank.astype(I32)

    parts, spread = tiles(slab, 0, 32)
    row_sym = matmul(parts.astype(BF16), small(spread), NN).astype(I32) ^ occ_lane
    parts, spread = tiles(slab, (MY // O) * x, 16)
    out_sym = matmul(parts.astype(BF16), small(spread), NN).astype(I32) ^ occ_lane
    parts, _ = tiles(slab_energy, (MY // O) * x, 8)
    out_shift = occ_energy_lane - exact(parts, one_hot(spread), NN)
    out_sym = side_by_side(out_sym, 0, 6)[:, :MY]
    out_shift = side_by_side(out_shift, 0, 6)[:, :MY]

    parts, spread = tiles(virtual, (WIDE // O) * x, 48)
    columns = matmul(parts.astype(BF16), small(spread), NN).astype(I32) ^ occ_lane
    for n in range(38):
        w_sym[:, pl.ds(n * 128, 128)] = columns[n : n + 1]

    first_c, inside = (COLS * d) // O, (COLS * d) % O
    near = small(iota((n_virtual, 128), 0) == first_c + iota((n_virtual, 128), 1))
    near = matmul(jnp.broadcast_to(virtual, (16, n_virtual)).astype(BF16), near, NN)
    near_all = jnp.broadcast_to(near[:1], (128, 128)).astype(BF16)
    at = inside + iota((APAD, 128), 0)
    v_col = matmul(small((at >> 4) == iota((APAD, 128), 1)), near_all, NT).astype(I32)
    at = inside + iota((APAD, O), 0)
    o_col = matmul(small((at & 15) == iota((APAD, O), 1)), occ_all, NT).astype(I32)
    a_col_sym = (v_col ^ o_col)[:COLS, :1]
    at = inside + iota((128, 384), 1)
    v_row = matmul(near_all[:16], small((at >> 4) == iota((128, 384), 0)), NN)[:1].astype(I32)
    at = inside + iota((O, 384), 1)
    pick_o = small((at & 15) == iota((O, 384), 0))
    o_row = matmul(occ_all[:16], pick_o, NN)[:1].astype(I32)
    rank_all = jnp.broadcast_to(rank[:, :O], (16, O)).astype(BF16)
    rank_row = matmul(rank_all, pick_o, NN)[:1].astype(I32)
    at = inside + iota((1, 384), 1)
    a_code = SLOTS * ((v_row ^ o_row) - 2 * x) + 2 * (at >> 4) + rank_row
    a_code = jnp.where(iota((1, 384), 1) < COLS, a_code, -1)[:, :APAD]

    at = BJ * d + iota((BPAD, n_slab), 0)
    pick_b = (at >> 4) == iota((BPAD, n_slab), 1)
    at = BJ * d + iota((BPAD, O), 0)
    pick_j = (at & 15) == iota((BPAD, O), 1)
    bj_col = matmul(small(pick_b), slab_all, NT).astype(I32) ^ matmul(
        small(pick_j), occ_all, NT
    ).astype(I32)
    bj_sym = jnp.where(iota((BPAD, 128), 0) < BJ, bj_col, -1)
    bj_shift = (
        exact(one_hot(pick_j), jnp.broadcast_to(occupied_energy, (128, O)), NT)
        - exact(one_hot(pick_b), jnp.broadcast_to(slab_energy, (128, n_slab)), NT)
    )[:, :1]
    at = BJ * d + iota((n_slab, 128), 1)
    b_row = matmul(slab_all[:16], small((at >> 4) == iota((n_slab, 128), 0)), NN)[:1]
    at = BJ * d + iota((O, 128), 1)
    j_row = matmul(occ_all[:16], small((at & 15) == iota((O, 128), 0)), NN)[:1]
    bj_row = jnp.where(iota((1, 128), 1) < BJ, b_row.astype(I32) ^ j_row.astype(I32), -1)
    same = bj_sym == bj_row
    shape = (BPAD, 128)
    slot_row = jnp.sum(one_hot(same & (iota(shape, 0) < iota(shape, 1))), axis=0, keepdims=True)
    slot_col = jnp.sum(one_hot(same & (iota(shape, 1) < iota(shape, 0))), axis=1, keepdims=True)
    bj_code = jnp.where(bj_row < 0, -1, 8 * bj_row + slot_row.astype(I32))[:, :BPAD]
    bj_sym = bj_sym[:, :1]
    bj_code_col = jnp.where(bj_sym < 0, -1, 8 * bj_sym + slot_col.astype(I32))

    for n in range(16):
        pick[:, pl.ds(n * 128, 128)] = small(key + 16 * n == iota((256, 128), 0))
    for n in range(4):
        o_msg[n] = jnp.zeros((2, Z, 8, 128), F32)
        w_split[pl.ds(n * BPAD + 32, 16)] = jnp.zeros((16, 2432), BF16)
    for n in range(2):
        a_split[pl.ds(n * APAD + 288, 16)] = jnp.zeros((16, ROWS), BF16)

    load_w.wait()
    for half in range(2):
        cols = pl.ds(half * HALF, HALF)
        kept = jnp.where(bj_sym[:BJ] == w_sym[:, cols], w_in[:, cols], 0.0)
        high, low = halves(kept)
        w_split[pl.ds(half * 2 * BPAD, BJ), pl.ds(0, HALF)] = high
        w_split[pl.ds((half * 2 + 1) * BPAD, BJ), pl.ds(0, HALF)] = low
    w_main = matmul(w_split[:, pl.ds(0, 2048)], pick[...], NT)
    w_rest = matmul(
        w_split[:, pl.ds(2048, HALF - 2048)], pick[pl.ds(0, 128), pl.ds(0, HALF - 2048)], NT
    )
    group = small(iota((IRREPS * 8, BPAD), 0) == bj_code)
    for half in range(2):
        rows = [slice((2 * half + n) * BPAD, (2 * half + n + 1) * BPAD) for n in range(2)]
        main = sum(matmul(group, w_main[r].astype(BF16), NN) for r in rows)
        rest = sum(matmul(group, w_rest[r].astype(BF16), NN) for r in rows)
        w_msg[:, half, :, pl.ds(0, 256)] = main.reshape(IRREPS, 8, 256)
        w_msg[:, half, :, pl.ds(256, 128)] = rest.reshape(IRREPS, 8, 128)

    load_a.wait()
    for n in range(11):
        cols = pl.ds(n * 256, 256)
        kept = jnp.where(
            a_col_sym == side_by_side(row_sym, 2 * n, 2), a_in[:, cols], 0.0
        )
        high, low = halves(kept)
        a_split[pl.ds(0, COLS), cols] = high
        a_split[pl.ds(APAD, COLS), cols] = low
    a_main = matmul(a_split[:, pl.ds(0, 2048)], pick[...], NT)
    a_rest = matmul(
        a_split[:, pl.ds(2048, ROWS - 2048)], pick[pl.ds(0, 128), pl.ds(0, ROWS - 2048)], NT
    )
    place_rows = small(iota((2 * SLOTS, APAD), 0) == a_code)
    rows = [slice(n * APAD, (n + 1) * APAD) for n in range(2)]
    main = sum(matmul(place_rows, a_main[r].astype(BF16), NN) for r in rows)
    rest = sum(matmul(place_rows, a_rest[r].astype(BF16), NN) for r in rows)
    a_msg[:, :, pl.ds(0, 256)] = main.reshape(2, SLOTS, 256)
    a_msg[:, :, pl.ds(256, 128)] = rest.reshape(2, SLOTS, 128)

    pl.semaphore_wait(barrier, 6 + Z * PLACES - 1)

    sends = []

    def send(source, target, send_sem, recv_sem, dd, xx):
        copy = pltpu.make_async_remote_copy(
            src_ref=source,
            dst_ref=target,
            send_sem=send_sem,
            recv_sem=recv_sem,
            device_id=(dd, xx),
            device_id_type=MESH,
        )
        copy.start()
        sends.append(copy)

    for j in range(2):
        cs = core_at[j]
        for m in (2, 1, 3):
            send(
                w_msg.at[2 * x_at[m] + cs],
                w_mid.at[cs, x],
                x_send.at[3 * j + m - 1],
                x_recv.at[cs],
                d,
                x_at[m],
            )
        pltpu.make_async_copy(w_msg.at[2 * x + cs], w_mid.at[cs, x], x_recv.at[cs]).start()

    for m in (2, 1, 3, 0):
        for j in range(2):
            if m or j:
                send(
                    a_msg.at[core_at[j]],
                    a_got.at[place],
                    a_send.at[2 * m + j],
                    a_recv,
                    z * PLACES + y_at[m] * 2 + core_at[j],
                    x,
                )
    pltpu.make_async_copy(a_msg.at[core], a_got.at[place], a_recv).start()

    for j in range(2):
        ready = w_mid.at[core_at[j]]
        pltpu.make_async_copy(ready, ready, x_recv.at[core_at[j]]).wait()
        for n in FAR_FIRST:
            zs = z_at[n]
            if n or j:
                send(
                    ready.at[lax.div(zs, 2), lax.rem(zs, 2)],
                    w_got.at[j, z],
                    w_send.at[j, n],
                    w_recv.at[j],
                    zs * PLACES + here + core_at[j],
                    x,
                )
            else:
                pltpu.make_async_copy(
                    ready.at[lax.div(z, 2), lax.rem(z, 2)], w_got.at[0, z], w_recv.at[0]
                ).start()

    a_all[...] = jnp.zeros(a_all.shape, F32)
    pltpu.make_async_copy(a_got, a_got, a_recv).wait()
    for p in range(PLACES):
        first = 2 * START[p]
        a_all[pl.ds(first, SLOTS), :] += a_got[p]
    a_high, a_low = halves(a_all[...])
    slot_o = z * PLACES + 2 * x + core

    for j in range(2):
        pltpu.make_async_copy(w_got.at[j], w_got.at[j], w_recv.at[j]).wait()
        w_high, w_low = halves(w_got[j].reshape(Z * 8, 384))
        product = matmul(w_high, a_low, NN) + matmul(w_low, a_high, NN)
        product = product + matmul(w_high, a_high, NN)
        for part in range(X):
            o_msg[part, j, :, :, pl.ds(0, QA)] = product[:, part * QA : (part + 1) * QA].reshape(
                Z, 8, QA
            )

        for n in FAR_FIRST:
            for m in range(X):
                if n or m or j:
                    send(
                        o_msg.at[x_at[m], j, z_at[n]],
                        o_got.at[slot_o],
                        o_send.at[j, X * n + m],
                        o_recv,
                        z_at[n] * PLACES + here + core_at[j],
                        x_at[m],
                    )
                else:
                    pltpu.make_async_copy(o_msg.at[x, 0, z], o_got.at[slot_o], o_recv).start()

    spread = small((iota((BPAD, 128), 1) & 63) == bj_code_col)
    pltpu.make_async_copy(o_got, o_got, o_recv).wait()
    total = o_got[pl.ds(0, PLACES)]
    for zs in range(1, Z):
        total = total + o_got[pl.ds(zs * PLACES, PLACES)]
    high, low = halves(total.reshape(IRREPS * 8, 128))
    mine = matmul(spread, jnp.concatenate([high, low], axis=0), NN)
    high, low = halves(mine)
    widen = pick[pl.ds(0, 128), pl.ds(0, MY)]
    cycle = matmul(high, widen, NN) + matmul(low, widen, NN)
    value = jnp.where(bj_sym == out_sym, cycle, 0.0) / (out_shift + bj_shift)
    out_ref[...] = value[:BJ]

    for copy in sends:
        copy.wait_send()


def local(
    amplitudes, integrals, slab_irrep, virtual_irrep, occupied_irrep, occupied_energy, slab_energy
):
    vmem = pl.BlockSpec(memory_space=pltpu.VMEM)
    hbm = pl.BlockSpec(memory_space=pltpu.HBM)
    out = pl.pallas_call(
        kernel,
        out_shape=jax.ShapeDtypeStruct((BJ, MY), F32),
        in_specs=[hbm] * 7,
        out_specs=vmem,
        scratch_shapes=[
            pltpu.VMEM(slab_irrep.shape, I32),
            pltpu.VMEM(virtual_irrep.shape, I32),
            pltpu.VMEM(occupied_irrep.shape, I32),
            pltpu.VMEM(occupied_energy.shape, F32),
            pltpu.VMEM(slab_energy.shape, F32),
            pltpu.VMEM((COLS, ROWS), F32),
            pltpu.VMEM((BJ, WIDE), F32),
            pltpu.VMEM((2 * APAD, ROWS), BF16),
            pltpu.VMEM((4 * BPAD, 2432), BF16),
            pltpu.VMEM((256, 2048), BF16),
            pltpu.VMEM((2, SLOTS, 384), F32),
            pltpu.VMEM((IRREPS, 2, 8, 384), F32),
            pltpu.VMEM((2, X, 2, 8, 384), F32),
            pltpu.VMEM((PLACES, SLOTS, 384), F32),
            pltpu.VMEM((2, Z, 8, 384), F32),
            pltpu.VMEM((384, 384), F32),
            pltpu.VMEM((1, 38 * 128), I32),
            pltpu.VMEM((X, 2, Z, 8, 128), F32),
            pltpu.VMEM((Z * PLACES, 8, 128), F32),
            pltpu.SemaphoreType.DMA((7,)),
            pltpu.SemaphoreType.DMA((PLACES,)),
            pltpu.SemaphoreType.DMA((6,)),
            pltpu.SemaphoreType.DMA((2, Z)),
            pltpu.SemaphoreType.DMA((2, Z * X)),
            pltpu.SemaphoreType.DMA,
            pltpu.SemaphoreType.DMA((2,)),
            pltpu.SemaphoreType.DMA((2,)),
            pltpu.SemaphoreType.DMA,
        ],
        compiler_params=pltpu.CompilerParams(
            collective_id=0, has_side_effects=True, vmem_limit_bytes=58 << 20
        ),
    )(
        amplitudes.T,
        integrals,
        slab_irrep,
        virtual_irrep,
        occupied_irrep,
        occupied_energy,
        slab_energy,
    )
    return out.T


def solution(mesh):
    return jax.shard_map(
        local,
        mesh=mesh,
        in_specs=(P(None, "dist"), P("dist", "rep"), P(), P(), P(), P(), P()),
        out_specs=P("rep", "dist"),
        check_vma=False,
    )
```

```python
import jax
import jax.numpy as jnp
from jax import lax
from jax.experimental import pallas as pl
from jax.experimental.pallas import tpu as pltpu
from jax.sharding import PartitionSpec as P

MESH = pl.DeviceIdType.MESH
F32, BF16, I32 = jnp.float32, jnp.bfloat16, jnp.int32

O = 16
IRREPS = 8
Z, Y, X = 8, 4, 4
PLACES = 8
ROWS = 2816
COLS = 300
WIDE = 4800
HALF = 2400
BJ = 44
MY = 704
SLOTS = 40
QA = 88
APAD, BPAD = 304, 48
START = [(COLS * p) // O for p in range(PLACES)]


def halves(value):
    high = value.astype(BF16)
    return high, (value - high.astype(F32)).astype(BF16)


def matmul(left, right, dims):
    return lax.dot_general(left, right, (dims, ((), ())), preferred_element_type=F32)


NN = ((1,), (0,))
NT = ((1,), (1,))


def iota(shape, dim):
    return lax.broadcasted_iota(I32, shape, dim)


def exact(left, right, dims):
    return lax.dot_general(
        left, right, (dims, ((), ())), precision=lax.Precision.HIGHEST, preferred_element_type=F32
    )


def one_hot(mask):
    return mask.astype(F32)


def small(mask):
    return mask.astype(F32).astype(BF16)


def tiles(values, offset, count):
    size = values.shape[1]
    at = iota((count, size), 1) - offset
    parts = jnp.where((at >> 3) == iota((count, size), 0), values, 0.0)
    spread = ((iota((size, 128), 0) - offset) & 7) == (iota((size, 128), 1) >> 4)
    return parts, spread


FAR_FIRST = (4, 5, 3, 6, 2, 7, 1, 0)


def side_by_side(rows, first, count):
    return jnp.concatenate([rows[first + n : first + n + 1] for n in range(count)], axis=1)


def kernel(
    a_hbm,
    w_hbm,
    slab_hbm,
    virtual_hbm,
    occupied_hbm,
    occupied_energy_hbm,
    slab_energy_hbm,
    out_ref,
    slab_ref,
    virtual_ref,
    occupied_ref,
    occupied_energy_ref,
    slab_energy_ref,
    a_in,
    w_in,
    a_split,
    w_split,
    pick,
    a_msg,
    w_msg,
    w_mid,
    a_got,
    w_got,
    a_all,
    w_sym,
    o_msg,
    o_got,
    o_sum,
    load_sem,
    a_send,
    x_send,
    w_send,
    o_send,
    a_recv,
    x_recv,
    w_recv,
    o_recv,
):
    d = lax.axis_index("dist")
    x = lax.axis_index("rep")
    z, place = lax.div(d, PLACES), lax.rem(d, PLACES)
    y, core = lax.div(place, 2), lax.rem(place, 2)
    z_at = [lax.rem(z + n, Z) for n in range(Z)]
    y_at = [lax.rem(y + n, Y) for n in range(Y)]
    x_at = [lax.rem(x + n, X) for n in range(X)]
    core_at = [core, 1 - core]
    here = y * 2
    load_a = pltpu.make_async_copy(a_hbm, a_in, load_sem.at[0])
    load_w = pltpu.make_async_copy(w_hbm, w_in, load_sem.at[1])
    loads = [
        pltpu.make_async_copy(source, target, load_sem.at[2 + n])
        for n, (source, target) in enumerate(
            [
                (occupied_hbm, occupied_ref),
                (slab_hbm, slab_ref),
                (virtual_hbm, virtual_ref),
                (occupied_energy_hbm, occupied_energy_ref),
                (slab_energy_hbm, slab_energy_ref),
            ]
        )
    ]
    for load in loads:
        load.start()
    load_w.start()
    load_a.start()

    barrier = pltpu.get_barrier_semaphore()

    def greet(dd, xx):
        pl.semaphore_signal(barrier, inc=1, device_id=(dd, xx), device_id_type=MESH)

    for n in FAR_FIRST:
        for m in range(X):
            for j in range(2):
                if n or m or j:
                    greet(z_at[n] * PLACES + here + core_at[j], x_at[m])
    for m in range(1, Y):
        for j in range(2):
            greet(z * PLACES + y_at[m] * 2 + core_at[j], x)

    for load in loads:
        load.wait()
    slab = slab_ref[...].reshape(1, -1).astype(F32)
    virtual = virtual_ref[...].reshape(1, -1).astype(F32)
    occupied = occupied_ref[...].reshape(1, -1).astype(F32)
    occupied_energy = occupied_energy_ref[...].reshape(1, -1)
    slab_energy = slab_energy_ref[...].reshape(1, -1)
    n_slab, n_virtual = slab.shape[1], virtual.shape[1]
    slab_all = jnp.broadcast_to(slab, (128, n_slab)).astype(BF16)
    occ_all = jnp.broadcast_to(occupied, (128, O)).astype(BF16)

    repeat = iota((O, 128), 0) == (iota((O, 128), 1) & 15)
    occ_lane = matmul(occ_all[:16], small(repeat), NN)[:1].astype(I32)
    occ_energy_lane = exact(jnp.broadcast_to(occupied_energy, (8, O)), one_hot(repeat), NN)[:1]
    occ_col = matmul(small(iota((O, O), 0) == iota((O, O), 1)), occ_all, NT).astype(I32)
    earlier = (occ_col == occ_lane) & (iota((O, 128), 0) < (iota((O, 128), 1) & 15))
    rank = jnp.sum(one_hot(earlier), axis=0, keepdims=True)
    key = 2 * (iota((1, 128), 1) >> 4) + rank.astype(I32)

    parts, spread = tiles(slab, 0, 32)
    row_sym = matmul(parts.astype(BF16), small(spread), NN).astype(I32) ^ occ_lane
    parts, spread = tiles(slab, (MY // O) * x, 16)
    out_sym = matmul(parts.astype(BF16), small(spread), NN).astype(I32) ^ occ_lane
    parts, _ = tiles(slab_energy, (MY // O) * x, 8)
    out_shift = occ_energy_lane - exact(parts, one_hot(spread), NN)
    out_sym = side_by_side(out_sym, 0, 6)[:, :MY]
    out_shift = side_by_side(out_shift, 0, 6)[:, :MY]

    parts, spread = tiles(virtual, (WIDE // O) * x, 48)
    columns = matmul(parts.astype(BF16), small(spread), NN).astype(I32) ^ occ_lane
    for n in range(38):
        w_sym[:, pl.ds(n * 128, 128)] = columns[n : n + 1]

    first_c, inside = (COLS * d) // O, (COLS * d) % O
    near = small(iota((n_virtual, 128), 0) == first_c + iota((n_virtual, 128), 1))
    near = matmul(jnp.broadcast_to(virtual, (16, n_virtual)).astype(BF16), near, NN)
    near_all = jnp.broadcast_to(near[:1], (128, 128)).astype(BF16)
    at = inside + iota((APAD, 128), 0)
    v_col = matmul(small((at >> 4) == iota((APAD, 128), 1)), near_all, NT).astype(I32)
    at = inside + iota((APAD, O), 0)
    o_col = matmul(small((at & 15) == iota((APAD, O), 1)), occ_all, NT).astype(I32)
    a_col_sym = (v_col ^ o_col)[:COLS, :1]
    at = inside + iota((128, 384), 1)
    v_row = matmul(near_all[:16], small((at >> 4) == iota((128, 384), 0)), NN)[:1].astype(I32)
    at = inside + iota((O, 384), 1)
    pick_o = small((at & 15) == iota((O, 384), 0))
    o_row = matmul(occ_all[:16], pick_o, NN)[:1].astype(I32)
    rank_all = jnp.broadcast_to(rank[:, :O], (16, O)).astype(BF16)
    rank_row = matmul(rank_all, pick_o, NN)[:1].astype(I32)
    at = inside + iota((1, 384), 1)
    a_code = SLOTS * ((v_row ^ o_row) - 2 * x) + 2 * (at >> 4) + rank_row
    a_code = jnp.where(iota((1, 384), 1) < COLS, a_code, -1)[:, :APAD]

    at = BJ * d + iota((BPAD, n_slab), 0)
    pick_b = (at >> 4) == iota((BPAD, n_slab), 1)
    at = BJ * d + iota((BPAD, O), 0)
    pick_j = (at & 15) == iota((BPAD, O), 1)
    bj_col = matmul(small(pick_b), slab_all, NT).astype(I32) ^ matmul(
        small(pick_j), occ_all, NT
    ).astype(I32)
    bj_sym = jnp.where(iota((BPAD, 128), 0) < BJ, bj_col, -1)
    bj_shift = (
        exact(one_hot(pick_j), jnp.broadcast_to(occupied_energy, (128, O)), NT)
        - exact(one_hot(pick_b), jnp.broadcast_to(slab_energy, (128, n_slab)), NT)
    )[:, :1]
    at = BJ * d + iota((n_slab, 128), 1)
    b_row = matmul(slab_all[:16], small((at >> 4) == iota((n_slab, 128), 0)), NN)[:1]
    at = BJ * d + iota((O, 128), 1)
    j_row = matmul(occ_all[:16], small((at & 15) == iota((O, 128), 0)), NN)[:1]
    bj_row = jnp.where(iota((1, 128), 1) < BJ, b_row.astype(I32) ^ j_row.astype(I32), -1)
    same = bj_sym == bj_row
    shape = (BPAD, 128)
    slot_row = jnp.sum(one_hot(same & (iota(shape, 0) < iota(shape, 1))), axis=0, keepdims=True)
    slot_col = jnp.sum(one_hot(same & (iota(shape, 1) < iota(shape, 0))), axis=1, keepdims=True)
    bj_code = jnp.where(bj_row < 0, -1, 8 * bj_row + slot_row.astype(I32))[:, :BPAD]
    bj_sym = bj_sym[:, :1]
    bj_code_col = jnp.where(bj_sym < 0, -1, 8 * bj_sym + slot_col.astype(I32))

    for n in range(16):
        pick[:, pl.ds(n * 128, 128)] = small(key + 16 * n == iota((256, 128), 0))
    for n in range(4):
        w_split[pl.ds(n * BPAD + 32, 16)] = jnp.zeros((16, 2432), BF16)
    for n in range(2):
        a_split[pl.ds(n * APAD + 288, 16)] = jnp.zeros((16, ROWS), BF16)

    load_w.wait()
    for half in range(2):
        cols = pl.ds(half * HALF, HALF)
        kept = jnp.where(bj_sym[:BJ] == w_sym[:, cols], w_in[:, cols], 0.0)
        high, low = halves(kept)
        w_split[pl.ds(half * 2 * BPAD, BJ), pl.ds(0, HALF)] = high
        w_split[pl.ds((half * 2 + 1) * BPAD, BJ), pl.ds(0, HALF)] = low
    w_main = matmul(w_split[:, pl.ds(0, 2048)], pick[...], NT)
    w_rest = matmul(
        w_split[:, pl.ds(2048, HALF - 2048)], pick[pl.ds(0, 128), pl.ds(0, HALF - 2048)], NT
    )
    row = iota((IRREPS * 8, BPAD), 0)
    group = small(row == bj_code)
    row = row & 31
    row = 8 * (row >> 2) + (row & 3) + 4 * (iota((IRREPS * 8, BPAD), 0) >> 5)
    group_rest = small(row == bj_code)
    for half in range(2):
        rows = [slice((2 * half + n) * BPAD, (2 * half + n + 1) * BPAD) for n in range(2)]
        main = sum(matmul(group, w_main[r].astype(BF16), NN) for r in rows)
        rest = sum(matmul(group_rest, w_rest[r].astype(BF16), NN) for r in rows)
        w_msg[:, half, pl.ds(0, 8)] = main[:, :128].reshape(IRREPS, 8, 128)
        w_msg[:, half, pl.ds(8, 8)] = main[:, 128:].reshape(IRREPS, 8, 128)
        rest = rest[:32] + pltpu.roll(rest[32:], 64, 1)
        w_msg[:, half, pl.ds(16, 4)] = rest.reshape(IRREPS, 4, 128)

    load_a.wait()
    for n in range(11):
        cols = pl.ds(n * 256, 256)
        kept = jnp.where(
            a_col_sym == side_by_side(row_sym, 2 * n, 2), a_in[:, cols], 0.0
        )
        high, low = halves(kept)
        a_split[pl.ds(0, COLS), cols] = high
        a_split[pl.ds(APAD, COLS), cols] = low
    a_main = matmul(a_split[:, pl.ds(0, 2048)], pick[...], NT)
    a_rest = matmul(
        a_split[:, pl.ds(2048, ROWS - 2048)], pick[pl.ds(0, 128), pl.ds(0, ROWS - 2048)], NT
    )
    place_rows = small(iota((2 * SLOTS, APAD), 0) == a_code)
    rows = [slice(n * APAD, (n + 1) * APAD) for n in range(2)]
    main = sum(matmul(place_rows, a_main[r].astype(BF16), NN) for r in rows)
    rest = sum(matmul(place_rows, a_rest[r].astype(BF16), NN) for r in rows)
    a_msg[:, :, pl.ds(0, 256)] = main.reshape(2, SLOTS, 256)
    a_msg[:, :, pl.ds(256, 128)] = rest.reshape(2, SLOTS, 128)

    pl.semaphore_wait(barrier, 6 + Z * PLACES - 1)

    sends = []

    def send(source, target, send_sem, recv_sem, dd, xx):
        copy = pltpu.make_async_remote_copy(
            src_ref=source,
            dst_ref=target,
            send_sem=send_sem,
            recv_sem=recv_sem,
            device_id=(dd, xx),
            device_id_type=MESH,
        )
        copy.start()
        sends.append(copy)

    for j in range(2):
        cs = core_at[j]
        for m in (2, 1, 3):
            send(
                w_msg.at[2 * x_at[m] + cs],
                w_mid.at[cs, x],
                x_send.at[3 * j + m - 1],
                x_recv.at[cs],
                d,
                x_at[m],
            )
        pltpu.make_async_copy(w_msg.at[2 * x + cs], w_mid.at[cs, x], x_recv.at[cs]).start()

    for m in (2, 1, 3, 0):
        for j in range(2):
            if m or j:
                send(
                    a_msg.at[core_at[j]],
                    a_got.at[place],
                    a_send.at[2 * m + j],
                    a_recv,
                    z * PLACES + y_at[m] * 2 + core_at[j],
                    x,
                )
    pltpu.make_async_copy(a_msg.at[core], a_got.at[place], a_recv).start()

    for j in range(2):
        ready = w_mid.at[core_at[j]]
        pltpu.make_async_copy(ready, ready, x_recv.at[core_at[j]]).wait()
        for n in FAR_FIRST:
            zs = z_at[n]
            if n or j:
                send(
                    ready.at[lax.div(zs, 2), lax.rem(zs, 2)],
                    w_got.at[j, z],
                    w_send.at[j, n],
                    w_recv.at[j],
                    zs * PLACES + here + core_at[j],
                    x,
                )
            else:
                pltpu.make_async_copy(
                    ready.at[lax.div(z, 2), lax.rem(z, 2)], w_got.at[0, z], w_recv.at[0]
                ).start()

    a_all[...] = jnp.zeros(a_all.shape, F32)
    pltpu.make_async_copy(a_got, a_got, a_recv).wait()
    for p in range(PLACES):
        first = 2 * START[p]
        a_all[pl.ds(first, SLOTS), :] += a_got[p]
    a_high, a_low = halves(a_all[...])
    slot_o = z * PLACES + 2 * x + core

    for j in range(2):
        pltpu.make_async_copy(w_got.at[j], w_got.at[j], w_recv.at[j]).wait()
        rows = []
        for slot in range(8):
            tail = w_got[j, :, 16 + slot % 4, :]
            if slot >= 4:
                tail = pltpu.roll(tail, 64, 1)
            rows.append(
                jnp.concatenate([w_got[j, :, slot, :], w_got[j, :, 8 + slot, :], tail], axis=1)
            )
        w_high, w_low = halves(jnp.concatenate(rows, axis=0))
        product = matmul(w_high, a_low, NN) + matmul(w_low, a_high, NN)
        product = product + matmul(w_high, a_high, NN)
        for part in range(X):
            lanes = product[:, part * QA : (part + 1) * QA]
            ends = []
            for slot in (6, 7):
                whole = lanes[8 * slot : 8 * slot + 8]
                ends.append([whole[:, :40], whole[:, 40:80], whole[:, 80:]])
            nothing = jnp.zeros((8, 32), F32)
            ends = [
                ends[0][0],
                ends[0][1],
                ends[1][0],
                ends[1][1],
                jnp.concatenate([ends[0][2], nothing], axis=1),
                jnp.concatenate([ends[1][2], nothing], axis=1),
            ]
            for slot in range(6):
                o_msg[part, j, :, slot, :] = jnp.concatenate(
                    [lanes[8 * slot : 8 * slot + 8], ends[slot]], axis=1
                )

        for n in FAR_FIRST:
            for m in range(X):
                if n or m or j:
                    send(
                        o_msg.at[x_at[m], j, z_at[n]],
                        o_got.at[slot_o],
                        o_send.at[j, X * n + m],
                        o_recv,
                        z_at[n] * PLACES + here + core_at[j],
                        x_at[m],
                    )
                else:
                    pltpu.make_async_copy(o_msg.at[x, 0, z], o_got.at[slot_o], o_recv).start()

    o_sum[...] = jnp.zeros(o_sum.shape, F32)
    source = iota((BPAD, 128), 1) & 63
    spread = small(source == bj_code_col)
    end_row = source & 7
    end_slot = jnp.where((end_row == 2) | (end_row == 3) | (end_row == 5), 7, 6)
    end_slot = jnp.where(end_row < 6, end_slot, 8)
    spread_ends = small((source & 56) + end_slot == bj_code_col)
    pltpu.make_async_copy(o_got, o_got, o_recv).wait()
    total = o_got[pl.ds(0, PLACES)]
    for zs in range(1, Z):
        total = total + o_got[pl.ds(zs * PLACES, PLACES)]
    o_sum[:, pl.ds(0, 6), :] = total
    total = o_sum[...].reshape(IRREPS * 8, 128)
    row, lane = iota((IRREPS * 8, 128), 0) & 7, iota((IRREPS * 8, 128), 1)
    first = jnp.where(((row == 0) | (row == 2)) & (lane < 40), pltpu.roll(total, 40, 1), 0.0)
    second = ((row == 1) | (row == 3)) & (lane >= 40) & (lane < 80)
    second = jnp.where(second, pltpu.roll(total, 80, 1), 0.0)
    third = ((row == 4) | (row == 5)) & (lane >= 80) & (lane < QA)
    third = jnp.where(third, pltpu.roll(total, 120, 1), 0.0)
    high, low = halves(total)
    mine = matmul(spread, jnp.concatenate([high, low], axis=0), NN)
    high, low = halves(first + second + third)
    mine = mine + matmul(spread_ends, jnp.concatenate([high, low], axis=0), NN)
    high, low = halves(mine)
    widen = pick[pl.ds(0, 128), pl.ds(0, MY)]
    cycle = matmul(high, widen, NN) + matmul(low, widen, NN)
    value = jnp.where(bj_sym == out_sym, cycle, 0.0) / (out_shift + bj_shift)
    out_ref[...] = value[:BJ]

    for copy in sends:
        copy.wait_send()


def local(
    amplitudes, integrals, slab_irrep, virtual_irrep, occupied_irrep, occupied_energy, slab_energy
):
    vmem = pl.BlockSpec(memory_space=pltpu.VMEM)
    hbm = pl.BlockSpec(memory_space=pltpu.HBM)
    out = pl.pallas_call(
        kernel,
        out_shape=jax.ShapeDtypeStruct((BJ, MY), F32),
        in_specs=[hbm] * 7,
        out_specs=vmem,
        scratch_shapes=[
            pltpu.VMEM(slab_irrep.shape, I32),
            pltpu.VMEM(virtual_irrep.shape, I32),
            pltpu.VMEM(occupied_irrep.shape, I32),
            pltpu.VMEM(occupied_energy.shape, F32),
            pltpu.VMEM(slab_energy.shape, F32),
            pltpu.VMEM((COLS, ROWS), F32),
            pltpu.VMEM((BJ, WIDE), F32),
            pltpu.VMEM((2 * APAD, ROWS), BF16),
            pltpu.VMEM((4 * BPAD, 2432), BF16),
            pltpu.VMEM((256, 2048), BF16),
            pltpu.VMEM((2, SLOTS, 384), F32),
            pltpu.VMEM((IRREPS, 2, 20, 128), F32),
            pltpu.VMEM((2, X, 2, 20, 128), F32),
            pltpu.VMEM((PLACES, SLOTS, 384), F32),
            pltpu.VMEM((2, Z, 20, 128), F32),
            pltpu.VMEM((384, 384), F32),
            pltpu.VMEM((1, 38 * 128), I32),
            pltpu.VMEM((X, 2, Z, 6, 128), F32),
            pltpu.VMEM((Z * PLACES, 6, 128), F32),
            pltpu.VMEM((IRREPS, 8, 128), F32),
            pltpu.SemaphoreType.DMA((7,)),
            pltpu.SemaphoreType.DMA((PLACES,)),
            pltpu.SemaphoreType.DMA((6,)),
            pltpu.SemaphoreType.DMA((2, Z)),
            pltpu.SemaphoreType.DMA((2, Z * X)),
            pltpu.SemaphoreType.DMA,
            pltpu.SemaphoreType.DMA((2,)),
            pltpu.SemaphoreType.DMA((2,)),
            pltpu.SemaphoreType.DMA,
        ],
        compiler_params=pltpu.CompilerParams(
            collective_id=0, has_side_effects=True, vmem_limit_bytes=58 << 20
        ),
    )(
        amplitudes.T,
        integrals,
        slab_irrep,
        virtual_irrep,
        occupied_irrep,
        occupied_energy,
        slab_energy,
    )
    return out.T


def solution(mesh):
    return jax.shard_map(
        local,
        mesh=mesh,
        in_specs=(P(None, "dist"), P("dist", "rep"), P(), P(), P(), P(), P()),
        out_specs=P("rep", "dist"),
        check_vma=False,
    )
```

```python
import jax
import jax.numpy as jnp
from jax import lax
from jax.experimental import pallas as pl
from jax.experimental.pallas import tpu as pltpu
from jax.sharding import PartitionSpec as P

MESH = pl.DeviceIdType.MESH
F32, BF16, I32 = jnp.float32, jnp.bfloat16, jnp.int32

O = 16
IRREPS = 8
Z, Y, X = 8, 4, 4
PLACES = 8
ROWS = 2816
COLS = 300
WIDE = 4800
HALF = 2400
BJ = 44
MY = 704
SLOTS = 40
QA = 88
APAD, BPAD = 304, 48
START = [(COLS * p) // O for p in range(PLACES)]


def halves(value):
    high = value.astype(BF16)
    return high, (value - high.astype(F32)).astype(BF16)


def matmul(left, right, dims):
    return lax.dot_general(left, right, (dims, ((), ())), preferred_element_type=F32)


NN = ((1,), (0,))
NT = ((1,), (1,))


def iota(shape, dim):
    return lax.broadcasted_iota(I32, shape, dim)


def exact(left, right, dims):
    return lax.dot_general(
        left, right, (dims, ((), ())), precision=lax.Precision.HIGHEST, preferred_element_type=F32
    )


def one_hot(mask):
    return mask.astype(F32)


def small(mask):
    return mask.astype(F32).astype(BF16)


def tiles(values, offset, count):
    size = values.shape[1]
    at = iota((count, size), 1) - offset
    parts = jnp.where((at >> 3) == iota((count, size), 0), values, 0.0)
    spread = ((iota((size, 128), 0) - offset) & 7) == (iota((size, 128), 1) >> 4)
    return parts, spread


FAR_FIRST = (4, 5, 3, 6, 2, 7, 1, 0)


def side_by_side(rows, first, count):
    return jnp.concatenate([rows[first + n : first + n + 1] for n in range(count)], axis=1)


def kernel(
    a_hbm,
    w_hbm,
    slab_hbm,
    virtual_hbm,
    occupied_hbm,
    occupied_energy_hbm,
    slab_energy_hbm,
    out_ref,
    slab_ref,
    virtual_ref,
    occupied_ref,
    occupied_energy_ref,
    slab_energy_ref,
    a_in,
    w_in,
    a_split,
    w_split,
    pick,
    a_msg,
    w_msg,
    w_mid,
    a_got,
    w_got,
    a_all,
    w_sym,
    o_msg,
    o_got,
    o_sum,
    load_sem,
    a_send,
    x_send,
    w_send,
    o_send,
    a_first,
    a_recv,
    x_recv,
    w_recv,
    o_recv,
):
    d = lax.axis_index("dist")
    x = lax.axis_index("rep")
    z, place = lax.div(d, PLACES), lax.rem(d, PLACES)
    y, core = lax.div(place, 2), lax.rem(place, 2)
    z_at = [lax.rem(z + n, Z) for n in range(Z)]
    y_at = [lax.rem(y + n, Y) for n in range(Y)]
    x_at = [lax.rem(x + n, X) for n in range(X)]
    core_at = [core, 1 - core]
    here = y * 2
    load_a = pltpu.make_async_copy(a_hbm, a_in, load_sem.at[0])
    load_w = pltpu.make_async_copy(w_hbm, w_in, load_sem.at[1])
    loads = [
        pltpu.make_async_copy(source, target, load_sem.at[2 + n])
        for n, (source, target) in enumerate(
            [
                (occupied_hbm, occupied_ref),
                (slab_hbm, slab_ref),
                (virtual_hbm, virtual_ref),
                (occupied_energy_hbm, occupied_energy_ref),
                (slab_energy_hbm, slab_energy_ref),
            ]
        )
    ]
    for load in loads:
        load.start()
    load_w.start()
    load_a.start()

    barrier = pltpu.get_barrier_semaphore()

    def greet(dd, xx):
        pl.semaphore_signal(barrier, inc=1, device_id=(dd, xx), device_id_type=MESH)

    for n in FAR_FIRST:
        for m in range(X):
            for j in range(2):
                if n or m or j:
                    greet(z_at[n] * PLACES + here + core_at[j], x_at[m])
    for m in range(1, Y):
        for j in range(2):
            greet(z * PLACES + y_at[m] * 2 + core_at[j], x)

    for load in loads:
        load.wait()
    slab = slab_ref[...].reshape(1, -1).astype(F32)
    virtual = virtual_ref[...].reshape(1, -1).astype(F32)
    occupied = occupied_ref[...].reshape(1, -1).astype(F32)
    occupied_energy = occupied_energy_ref[...].reshape(1, -1)
    slab_energy = slab_energy_ref[...].reshape(1, -1)
    n_slab, n_virtual = slab.shape[1], virtual.shape[1]
    slab_all = jnp.broadcast_to(slab, (128, n_slab)).astype(BF16)
    occ_all = jnp.broadcast_to(occupied, (128, O)).astype(BF16)

    repeat = iota((O, 128), 0) == (iota((O, 128), 1) & 15)
    occ_lane = matmul(occ_all[:16], small(repeat), NN)[:1].astype(I32)
    occ_col = matmul(small(iota((O, O), 0) == iota((O, O), 1)), occ_all, NT).astype(I32)
    earlier = (occ_col == occ_lane) & (iota((O, 128), 0) < (iota((O, 128), 1) & 15))
    rank = jnp.sum(one_hot(earlier), axis=0, keepdims=True)
    key = 2 * (iota((1, 128), 1) >> 4) + rank.astype(I32)

    parts, spread = tiles(slab, 0, 32)
    row_sym = matmul(parts.astype(BF16), small(spread), NN).astype(I32) ^ occ_lane
    parts, spread = tiles(virtual, (WIDE // O) * x, 48)
    columns = matmul(parts.astype(BF16), small(spread), NN).astype(I32) ^ occ_lane
    for n in range(38):
        w_sym[:, pl.ds(n * 128, 128)] = columns[n : n + 1]

    first_c, inside = (COLS * d) // O, (COLS * d) % O
    near = small(iota((n_virtual, 128), 0) == first_c + iota((n_virtual, 128), 1))
    near = matmul(jnp.broadcast_to(virtual, (16, n_virtual)).astype(BF16), near, NN)
    near_all = jnp.broadcast_to(near[:1], (128, 128)).astype(BF16)
    at = inside + iota((APAD, 128), 0)
    v_col = matmul(small((at >> 4) == iota((APAD, 128), 1)), near_all, NT).astype(I32)
    at = inside + iota((APAD, O), 0)
    o_col = matmul(small((at & 15) == iota((APAD, O), 1)), occ_all, NT).astype(I32)
    a_col_sym = (v_col ^ o_col)[:COLS, :1]
    at = inside + iota((128, 384), 1)
    v_row = matmul(near_all[:16], small((at >> 4) == iota((128, 384), 0)), NN)[:1].astype(I32)
    at = inside + iota((O, 384), 1)
    pick_o = small((at & 15) == iota((O, 384), 0))
    o_row = matmul(occ_all[:16], pick_o, NN)[:1].astype(I32)
    rank_all = jnp.broadcast_to(rank[:, :O], (16, O)).astype(BF16)
    rank_row = matmul(rank_all, pick_o, NN)[:1].astype(I32)
    at = inside + iota((1, 384), 1)
    a_code = SLOTS * ((v_row ^ o_row) - 2 * x) + 2 * (at >> 4) + rank_row
    a_code = jnp.where(iota((1, 384), 1) < COLS, a_code, -1)[:, :APAD]

    at = BJ * d + iota((BPAD, n_slab), 0)
    pick_b = (at >> 4) == iota((BPAD, n_slab), 1)
    at = BJ * d + iota((BPAD, O), 0)
    pick_j = (at & 15) == iota((BPAD, O), 1)
    bj_col = matmul(small(pick_b), slab_all, NT).astype(I32) ^ matmul(
        small(pick_j), occ_all, NT
    ).astype(I32)
    bj_sym = jnp.where(iota((BPAD, 128), 0) < BJ, bj_col, -1)
    at = BJ * d + iota((n_slab, 128), 1)
    b_row = matmul(slab_all[:16], small((at >> 4) == iota((n_slab, 128), 0)), NN)[:1]
    at = BJ * d + iota((O, 128), 1)
    j_row = matmul(occ_all[:16], small((at & 15) == iota((O, 128), 0)), NN)[:1]
    bj_row = jnp.where(iota((1, 128), 1) < BJ, b_row.astype(I32) ^ j_row.astype(I32), -1)
    same = bj_sym == bj_row
    shape = (BPAD, 128)
    slot_row = jnp.sum(one_hot(same & (iota(shape, 0) < iota(shape, 1))), axis=0, keepdims=True)
    bj_code = jnp.where(bj_row < 0, -1, 8 * bj_row + slot_row.astype(I32))[:, :BPAD]
    bj_sym = bj_sym[:, :1]

    pick[...] = jnp.zeros(pick.shape, BF16)
    one_tile = small(key == iota((16, 128), 0))
    for n in range(16):
        pick[pl.ds(16 * n, 16), pl.ds(n * 128, 128)] = one_tile
    for n in range(4):
        w_split[pl.ds(n * BPAD + 32, 16)] = jnp.zeros((16, 2432), BF16)
    for n in range(2):
        a_split[pl.ds(n * APAD + 288, 16)] = jnp.zeros((16, ROWS), BF16)

    load_w.wait()
    for half in range(2):
        cols = pl.ds(half * HALF, HALF)
        kept = jnp.where(bj_sym[:BJ] == w_sym[:, cols], w_in[:, cols], 0.0)
        high, low = halves(kept)
        w_split[pl.ds(half * 2 * BPAD, BJ), pl.ds(0, HALF)] = high
        w_split[pl.ds((half * 2 + 1) * BPAD, BJ), pl.ds(0, HALF)] = low
    w_main = matmul(w_split[:, pl.ds(0, 2048)], pick[...], NT)
    w_rest = matmul(
        w_split[:, pl.ds(2048, HALF - 2048)], pick[pl.ds(0, 128), pl.ds(0, HALF - 2048)], NT
    )
    row = iota((IRREPS * 8, BPAD), 0)
    group = small(row == bj_code)
    row = row & 31
    row = 8 * (row >> 2) + (row & 3) + 4 * (iota((IRREPS * 8, BPAD), 0) >> 5)
    group_rest = small(row == bj_code)
    for half in range(2):
        rows = [slice((2 * half + n) * BPAD, (2 * half + n + 1) * BPAD) for n in range(2)]
        main = sum(matmul(group, w_main[r].astype(BF16), NN) for r in rows)
        rest = sum(matmul(group_rest, w_rest[r].astype(BF16), NN) for r in rows)
        w_msg[:, half, pl.ds(0, 8)] = main[:, :128].reshape(IRREPS, 8, 128)
        w_msg[:, half, pl.ds(8, 8)] = main[:, 128:].reshape(IRREPS, 8, 128)
        rest = rest[:32] + pltpu.roll(rest[32:], 64, 1)
        w_msg[:, half, pl.ds(16, 4)] = rest.reshape(IRREPS, 4, 128)

    load_a.wait()
    for n in range(11):
        cols = pl.ds(n * 256, 256)
        kept = jnp.where(
            a_col_sym == side_by_side(row_sym, 2 * n, 2), a_in[:, cols], 0.0
        )
        high, low = halves(kept)
        a_split[pl.ds(0, COLS), cols] = high
        a_split[pl.ds(APAD, COLS), cols] = low
    a_main = matmul(a_split[:, pl.ds(0, 2048)], pick[...], NT)
    a_rest = matmul(
        a_split[:, pl.ds(2048, ROWS - 2048)], pick[pl.ds(0, 128), pl.ds(0, ROWS - 2048)], NT
    )
    place_rows = small(iota((2 * SLOTS, APAD), 0) == a_code)
    rows = [slice(n * APAD, (n + 1) * APAD) for n in range(2)]
    main = sum(matmul(place_rows, a_main[r].astype(BF16), NN) for r in rows)
    rest = sum(matmul(place_rows, a_rest[r].astype(BF16), NN) for r in rows)
    a_msg[:, :, pl.ds(0, 256)] = main.reshape(2, SLOTS, 256)
    a_msg[:, :, pl.ds(256, 128)] = rest.reshape(2, SLOTS, 128)

    pl.semaphore_wait(barrier, 6 + Z * PLACES - 1)

    sends = []

    def send(source, target, send_sem, recv_sem, dd, xx):
        copy = pltpu.make_async_remote_copy(
            src_ref=source,
            dst_ref=target,
            send_sem=send_sem,
            recv_sem=recv_sem,
            device_id=(dd, xx),
            device_id_type=MESH,
        )
        copy.start()
        sends.append(copy)

    for j in range(2):
        cs = core_at[j]
        for m in (2, 1, 3):
            send(
                w_msg.at[2 * x_at[m] + cs],
                w_mid.at[cs, x],
                x_send.at[3 * j + m - 1],
                x_recv.at[cs],
                d,
                x_at[m],
            )
        pltpu.make_async_copy(w_msg.at[2 * x + cs], w_mid.at[cs, x], x_recv.at[cs]).start()

    for m in (3, 1, 2, 0):
        for j in range(2):
            if (m or j) and not (m == 2 and j):
                send(
                    a_msg.at[core_at[j]],
                    a_got.at[place],
                    a_send.at[2 * m + j],
                    a_first if m == 3 and j else a_recv,
                    z * PLACES + y_at[m] * 2 + core_at[j],
                    x,
                )
    pltpu.make_async_copy(a_msg.at[core], a_got.at[place], a_recv).start()

    occ_energy_lane = exact(jnp.broadcast_to(occupied_energy, (8, O)), one_hot(repeat), NN)[:1]
    parts, spread = tiles(slab, (MY // O) * x, 16)
    out_sym = matmul(parts.astype(BF16), small(spread), NN).astype(I32) ^ occ_lane
    parts, _ = tiles(slab_energy, (MY // O) * x, 8)
    out_shift = occ_energy_lane - exact(parts, one_hot(spread), NN)
    out_sym = side_by_side(out_sym, 0, 6)[:, :MY]
    out_shift = side_by_side(out_shift, 0, 6)[:, :MY]

    bj_shift = (
        exact(one_hot(pick_j), jnp.broadcast_to(occupied_energy, (128, O)), NT)
        - exact(one_hot(pick_b), jnp.broadcast_to(slab_energy, (128, n_slab)), NT)
    )[:, :1]
    slot_col = jnp.sum(one_hot(same & (iota(shape, 1) < iota(shape, 0))), axis=1, keepdims=True)
    bj_code_col = jnp.where(bj_sym < 0, -1, 8 * bj_sym + slot_col.astype(I32))

    for j in range(2):
        ready = w_mid.at[core_at[j]]
        pltpu.make_async_copy(ready, ready, x_recv.at[core_at[j]]).wait()
        for n in FAR_FIRST:
            zs = z_at[n]
            if n or j:
                send(
                    ready.at[lax.div(zs, 2), lax.rem(zs, 2)],
                    w_got.at[j, z],
                    w_send.at[j, n],
                    w_recv.at[j],
                    zs * PLACES + here + core_at[j],
                    x,
                )
            else:
                pltpu.make_async_copy(
                    ready.at[lax.div(z, 2), lax.rem(z, 2)], w_got.at[0, z], w_recv.at[0]
                ).start()

    passed = a_got.at[y_at[1] * 2 + core_at[1]]
    pltpu.make_async_copy(passed, passed, a_first).wait()
    send(passed, passed, a_send.at[5], a_recv, z * PLACES + y_at[3] * 2 + core, x)

    a_all[...] = jnp.zeros(a_all.shape, F32)
    others = a_got.at[pl.ds(0, PLACES - 1)]
    pltpu.make_async_copy(others, others, a_recv).wait()
    for p in range(PLACES):
        first = 2 * START[p]
        a_all[pl.ds(first, SLOTS), :] += a_got[p]
    a_high, a_low = halves(a_all[...])
    slot_o = z * PLACES + 2 * x + core

    for j in range(2):
        pltpu.make_async_copy(w_got.at[j], w_got.at[j], w_recv.at[j]).wait()
        rows = []
        for slot in range(8):
            tail = w_got[j, :, 16 + slot % 4, :]
            if slot >= 4:
                tail = pltpu.roll(tail, 64, 1)
            rows.append(
                jnp.concatenate([w_got[j, :, slot, :], w_got[j, :, 8 + slot, :], tail], axis=1)
            )
        w_high, w_low = halves(jnp.concatenate(rows, axis=0))
        product = matmul(w_high, a_low, NN) + matmul(w_low, a_high, NN)
        product = product + matmul(w_high, a_high, NN)
        for part in range(X):
            lanes = product[:, part * QA : (part + 1) * QA]
            ends = []
            for slot in (6, 7):
                whole = lanes[8 * slot : 8 * slot + 8]
                ends.append([whole[:, :40], whole[:, 40:80], whole[:, 80:]])
            nothing = jnp.zeros((8, 32), F32)
            ends = [
                ends[0][0],
                ends[0][1],
                ends[1][0],
                ends[1][1],
                jnp.concatenate([ends[0][2], nothing], axis=1),
                jnp.concatenate([ends[1][2], nothing], axis=1),
            ]
            for slot in range(6):
                o_msg[part, j, :, slot, :] = jnp.concatenate(
                    [lanes[8 * slot : 8 * slot + 8], ends[slot]], axis=1
                )

        for n in FAR_FIRST:
            for m in range(X):
                if n or m or j:
                    send(
                        o_msg.at[x_at[m], j, z_at[n]],
                        o_got.at[slot_o],
                        o_send.at[j, X * n + m],
                        o_recv,
                        z_at[n] * PLACES + here + core_at[j],
                        x_at[m],
                    )
                else:
                    pltpu.make_async_copy(o_msg.at[x, 0, z], o_got.at[slot_o], o_recv).start()

    o_sum[...] = jnp.zeros(o_sum.shape, F32)
    source = iota((BPAD, 128), 1) & 63
    spread = small(source == bj_code_col)
    end_row = source & 7
    end_slot = jnp.where((end_row == 2) | (end_row == 3) | (end_row == 5), 7, 6)
    end_slot = jnp.where(end_row < 6, end_slot, 8)
    spread_ends = small((source & 56) + end_slot == bj_code_col)
    pltpu.make_async_copy(o_got, o_got, o_recv).wait()
    total = o_got[pl.ds(0, PLACES)]
    for zs in range(1, Z):
        total = total + o_got[pl.ds(zs * PLACES, PLACES)]
    o_sum[:, pl.ds(0, 6), :] = total
    total = o_sum[...].reshape(IRREPS * 8, 128)
    row, lane = iota((IRREPS * 8, 128), 0) & 7, iota((IRREPS * 8, 128), 1)
    first = jnp.where(((row == 0) | (row == 2)) & (lane < 40), pltpu.roll(total, 40, 1), 0.0)
    second = ((row == 1) | (row == 3)) & (lane >= 40) & (lane < 80)
    second = jnp.where(second, pltpu.roll(total, 80, 1), 0.0)
    third = ((row == 4) | (row == 5)) & (lane >= 80) & (lane < QA)
    third = jnp.where(third, pltpu.roll(total, 120, 1), 0.0)
    high, low = halves(total)
    mine = matmul(spread, jnp.concatenate([high, low], axis=0), NN)
    high, low = halves(first + second + third)
    mine = mine + matmul(spread_ends, jnp.concatenate([high, low], axis=0), NN)
    high, low = halves(mine)
    widen = pick[pl.ds(0, 128), pl.ds(0, MY)]
    cycle = matmul(high, widen, NN) + matmul(low, widen, NN)
    value = jnp.where(bj_sym == out_sym, cycle, 0.0) / (out_shift + bj_shift)
    out_ref[...] = value[:BJ]

    for copy in sends:
        copy.wait_send()


def local(
    amplitudes, integrals, slab_irrep, virtual_irrep, occupied_irrep, occupied_energy, slab_energy
):
    vmem = pl.BlockSpec(memory_space=pltpu.VMEM)
    hbm = pl.BlockSpec(memory_space=pltpu.HBM)
    out = pl.pallas_call(
        kernel,
        out_shape=jax.ShapeDtypeStruct((BJ, MY), F32),
        in_specs=[hbm] * 7,
        out_specs=vmem,
        scratch_shapes=[
            pltpu.VMEM(slab_irrep.shape, I32),
            pltpu.VMEM(virtual_irrep.shape, I32),
            pltpu.VMEM(occupied_irrep.shape, I32),
            pltpu.VMEM(occupied_energy.shape, F32),
            pltpu.VMEM(slab_energy.shape, F32),
            pltpu.VMEM((COLS, ROWS), F32),
            pltpu.VMEM((BJ, WIDE), F32),
            pltpu.VMEM((2 * APAD, ROWS), BF16),
            pltpu.VMEM((4 * BPAD, 2432), BF16),
            pltpu.VMEM((256, 2048), BF16),
            pltpu.VMEM((2, SLOTS, 384), F32),
            pltpu.VMEM((IRREPS, 2, 20, 128), F32),
            pltpu.VMEM((2, X, 2, 20, 128), F32),
            pltpu.VMEM((PLACES, SLOTS, 384), F32),
            pltpu.VMEM((2, Z, 20, 128), F32),
            pltpu.VMEM((384, 384), F32),
            pltpu.VMEM((1, 38 * 128), I32),
            pltpu.VMEM((X, 2, Z, 6, 128), F32),
            pltpu.VMEM((Z * PLACES, 6, 128), F32),
            pltpu.VMEM((IRREPS, 8, 128), F32),
            pltpu.SemaphoreType.DMA((7,)),
            pltpu.SemaphoreType.DMA((PLACES,)),
            pltpu.SemaphoreType.DMA((6,)),
            pltpu.SemaphoreType.DMA((2, Z)),
            pltpu.SemaphoreType.DMA((2, Z * X)),
            pltpu.SemaphoreType.DMA,
            pltpu.SemaphoreType.DMA,
            pltpu.SemaphoreType.DMA((2,)),
            pltpu.SemaphoreType.DMA((2,)),
            pltpu.SemaphoreType.DMA,
        ],
        compiler_params=pltpu.CompilerParams(
            collective_id=0, has_side_effects=True, vmem_limit_bytes=58 << 20
        ),
    )(
        amplitudes.T,
        integrals,
        slab_irrep,
        virtual_irrep,
        occupied_irrep,
        occupied_energy,
        slab_energy,
    )
    return out.T


def solution(mesh):
    return jax.shard_map(
        local,
        mesh=mesh,
        in_specs=(P(None, "dist"), P("dist", "rep"), P(), P(), P(), P(), P()),
        out_specs=P("rep", "dist"),
        check_vma=False,
    )
```

```python
import jax
import jax.numpy as jnp
from jax import lax
from jax.experimental import pallas as pl
from jax.experimental.pallas import tpu as pltpu
from jax.sharding import PartitionSpec as P

MESH = pl.DeviceIdType.MESH
F32, BF16, I32 = jnp.float32, jnp.bfloat16, jnp.int32

O = 16
IRREPS = 8
Z, Y, X = 8, 4, 4
PLACES = 8
ROWS = 2816
COLS = 300
WIDE = 4800
HALF = 2400
BJ = 44
MY = 704
SLOTS = 40
QA = 88
APAD, BPAD = 304, 48
START = [(COLS * p) // O for p in range(PLACES)]


def halves(value):
    high = value.astype(BF16)
    return high, (value - high.astype(F32)).astype(BF16)


def matmul(left, right, dims):
    return lax.dot_general(left, right, (dims, ((), ())), preferred_element_type=F32)


NN = ((1,), (0,))
NT = ((1,), (1,))


def iota(shape, dim):
    return lax.broadcasted_iota(I32, shape, dim)


def exact(left, right, dims):
    return lax.dot_general(
        left, right, (dims, ((), ())), precision=lax.Precision.HIGHEST, preferred_element_type=F32
    )


def one_hot(mask):
    return mask.astype(F32)


def small(mask):
    return mask.astype(F32).astype(BF16)


def tiles(values, offset, count):
    size = values.shape[1]
    at = iota((count, size), 1) - offset
    parts = jnp.where((at >> 3) == iota((count, size), 0), values, 0.0)
    spread = ((iota((size, 128), 0) - offset) & 7) == (iota((size, 128), 1) >> 4)
    return parts, spread


FAR_FIRST = (4, 5, 3, 6, 2, 7, 1, 0)


def side_by_side(rows, first, count):
    return jnp.concatenate([rows[first + n : first + n + 1] for n in range(count)], axis=1)


def kernel(
    a_hbm,
    w_hbm,
    slab_hbm,
    virtual_hbm,
    occupied_hbm,
    occupied_energy_hbm,
    slab_energy_hbm,
    out_ref,
    slab_ref,
    virtual_ref,
    occupied_ref,
    occupied_energy_ref,
    slab_energy_ref,
    a_in,
    w_in,
    a_split,
    w_split,
    pick,
    a_msg,
    w_msg,
    w_mid,
    a_got,
    w_got,
    a_all,
    w_sym,
    o_msg,
    o_pass,
    o_got,
    o_sum,
    load_sem,
    a_send,
    x_send,
    w_send,
    o_send,
    a_first,
    a_recv,
    x_recv,
    w_recv,
    o_recv,
    pass_send,
    pass_recv,
):
    d = lax.axis_index("dist")
    x = lax.axis_index("rep")
    z, place = lax.div(d, PLACES), lax.rem(d, PLACES)
    y, core = lax.div(place, 2), lax.rem(place, 2)
    z_at = [lax.rem(z + n, Z) for n in range(Z)]
    y_at = [lax.rem(y + n, Y) for n in range(Y)]
    x_at = [lax.rem(x + n, X) for n in range(X)]
    core_at = [core, 1 - core]
    here = y * 2
    load_a = pltpu.make_async_copy(a_hbm, a_in, load_sem.at[0])
    load_w = pltpu.make_async_copy(w_hbm, w_in, load_sem.at[1])
    loads = [
        pltpu.make_async_copy(source, target, load_sem.at[2 + n])
        for n, (source, target) in enumerate(
            [
                (occupied_hbm, occupied_ref),
                (slab_hbm, slab_ref),
                (virtual_hbm, virtual_ref),
                (occupied_energy_hbm, occupied_energy_ref),
                (slab_energy_hbm, slab_energy_ref),
            ]
        )
    ]
    for load in loads:
        load.start()
    load_w.start()
    load_a.start()

    barrier = pltpu.get_barrier_semaphore()

    def greet(dd, xx):
        pl.semaphore_signal(barrier, inc=1, device_id=(dd, xx), device_id_type=MESH)

    for n in FAR_FIRST:
        for m in range(X):
            for j in range(2):
                if n or m or j:
                    greet(z_at[n] * PLACES + here + core_at[j], x_at[m])
    for m in range(1, Y):
        for j in range(2):
            greet(z * PLACES + y_at[m] * 2 + core_at[j], x)

    for load in loads:
        load.wait()
    slab = slab_ref[...].reshape(1, -1).astype(F32)
    virtual = virtual_ref[...].reshape(1, -1).astype(F32)
    occupied = occupied_ref[...].reshape(1, -1).astype(F32)
    occupied_energy = occupied_energy_ref[...].reshape(1, -1)
    slab_energy = slab_energy_ref[...].reshape(1, -1)
    n_slab, n_virtual = slab.shape[1], virtual.shape[1]
    slab_all = jnp.broadcast_to(slab, (128, n_slab)).astype(BF16)
    occ_all = jnp.broadcast_to(occupied, (128, O)).astype(BF16)

    repeat = iota((O, 128), 0) == (iota((O, 128), 1) & 15)
    occ_lane = matmul(occ_all[:16], small(repeat), NN)[:1].astype(I32)
    occ_col = matmul(small(iota((O, O), 0) == iota((O, O), 1)), occ_all, NT).astype(I32)
    earlier = (occ_col == occ_lane) & (iota((O, 128), 0) < (iota((O, 128), 1) & 15))
    rank = jnp.sum(one_hot(earlier), axis=0, keepdims=True)
    key = 2 * (iota((1, 128), 1) >> 4) + rank.astype(I32)

    parts, spread = tiles(slab, 0, 32)
    row_sym = matmul(parts.astype(BF16), small(spread), NN).astype(I32) ^ occ_lane
    parts, spread = tiles(virtual, (WIDE // O) * x, 48)
    columns = matmul(parts.astype(BF16), small(spread), NN).astype(I32) ^ occ_lane
    for n in range(38):
        w_sym[:, pl.ds(n * 128, 128)] = columns[n : n + 1]

    first_c, inside = (COLS * d) // O, (COLS * d) % O
    near = small(iota((n_virtual, 128), 0) == first_c + iota((n_virtual, 128), 1))
    near = matmul(jnp.broadcast_to(virtual, (16, n_virtual)).astype(BF16), near, NN)
    near_all = jnp.broadcast_to(near[:1], (128, 128)).astype(BF16)
    at = inside + iota((APAD, 128), 0)
    v_col = matmul(small((at >> 4) == iota((APAD, 128), 1)), near_all, NT).astype(I32)
    at = inside + iota((APAD, O), 0)
    o_col = matmul(small((at & 15) == iota((APAD, O), 1)), occ_all, NT).astype(I32)
    a_col_sym = (v_col ^ o_col)[:COLS, :1]
    at = inside + iota((128, 384), 1)
    v_row = matmul(near_all[:16], small((at >> 4) == iota((128, 384), 0)), NN)[:1].astype(I32)
    at = inside + iota((O, 384), 1)
    pick_o = small((at & 15) == iota((O, 384), 0))
    o_row = matmul(occ_all[:16], pick_o, NN)[:1].astype(I32)
    rank_all = jnp.broadcast_to(rank[:, :O], (16, O)).astype(BF16)
    rank_row = matmul(rank_all, pick_o, NN)[:1].astype(I32)
    at = inside + iota((1, 384), 1)
    a_code = SLOTS * ((v_row ^ o_row) - 2 * x) + 2 * (at >> 4) + rank_row
    a_code = jnp.where(iota((1, 384), 1) < COLS, a_code, -1)[:, :APAD]

    at = BJ * d + iota((BPAD, n_slab), 0)
    pick_b = (at >> 4) == iota((BPAD, n_slab), 1)
    at = BJ * d + iota((BPAD, O), 0)
    pick_j = (at & 15) == iota((BPAD, O), 1)
    bj_col = matmul(small(pick_b), slab_all, NT).astype(I32) ^ matmul(
        small(pick_j), occ_all, NT
    ).astype(I32)
    bj_sym = jnp.where(iota((BPAD, 128), 0) < BJ, bj_col, -1)
    at = BJ * d + iota((n_slab, 128), 1)
    b_row = matmul(slab_all[:16], small((at >> 4) == iota((n_slab, 128), 0)), NN)[:1]
    at = BJ * d + iota((O, 128), 1)
    j_row = matmul(occ_all[:16], small((at & 15) == iota((O, 128), 0)), NN)[:1]
    bj_row = jnp.where(iota((1, 128), 1) < BJ, b_row.astype(I32) ^ j_row.astype(I32), -1)
    same = bj_sym == bj_row
    shape = (BPAD, 128)
    slot_row = jnp.sum(one_hot(same & (iota(shape, 0) < iota(shape, 1))), axis=0, keepdims=True)
    bj_code = jnp.where(bj_row < 0, -1, 8 * bj_row + slot_row.astype(I32))[:, :BPAD]
    bj_sym = bj_sym[:, :1]

    pick[...] = jnp.zeros(pick.shape, BF16)
    one_tile = small(key == iota((16, 128), 0))
    for n in range(16):
        pick[pl.ds(16 * n, 16), pl.ds(n * 128, 128)] = one_tile
    for n in range(4):
        w_split[pl.ds(n * BPAD + 32, 16)] = jnp.zeros((16, 2432), BF16)
    for n in range(2):
        a_split[pl.ds(n * APAD + 288, 16)] = jnp.zeros((16, ROWS), BF16)

    load_w.wait()
    for half in range(2):
        cols = pl.ds(half * HALF, HALF)
        kept = jnp.where(bj_sym[:BJ] == w_sym[:, cols], w_in[:, cols], 0.0)
        high, low = halves(kept)
        w_split[pl.ds(half * 2 * BPAD, BJ), pl.ds(0, HALF)] = high
        w_split[pl.ds((half * 2 + 1) * BPAD, BJ), pl.ds(0, HALF)] = low
    w_main = matmul(w_split[:, pl.ds(0, 2048)], pick[...], NT)
    w_rest = matmul(
        w_split[:, pl.ds(2048, HALF - 2048)], pick[pl.ds(0, 128), pl.ds(0, HALF - 2048)], NT
    )
    row = iota((IRREPS * 8, BPAD), 0)
    group = small(row == bj_code)
    row = row & 31
    row = 8 * (row >> 2) + (row & 3) + 4 * (iota((IRREPS * 8, BPAD), 0) >> 5)
    group_rest = small(row == bj_code)
    for half in range(2):
        rows = [slice((2 * half + n) * BPAD, (2 * half + n + 1) * BPAD) for n in range(2)]
        main = sum(matmul(group, w_main[r].astype(BF16), NN) for r in rows)
        rest = sum(matmul(group_rest, w_rest[r].astype(BF16), NN) for r in rows)
        w_msg[:, half, pl.ds(0, 8)] = main[:, :128].reshape(IRREPS, 8, 128)
        w_msg[:, half, pl.ds(8, 8)] = main[:, 128:].reshape(IRREPS, 8, 128)
        rest = rest[:32] + pltpu.roll(rest[32:], 64, 1)
        w_msg[:, half, pl.ds(16, 4)] = rest.reshape(IRREPS, 4, 128)

    load_a.wait()
    for n in range(11):
        cols = pl.ds(n * 256, 256)
        kept = jnp.where(
            a_col_sym == side_by_side(row_sym, 2 * n, 2), a_in[:, cols], 0.0
        )
        high, low = halves(kept)
        a_split[pl.ds(0, COLS), cols] = high
        a_split[pl.ds(APAD, COLS), cols] = low
    a_main = matmul(a_split[:, pl.ds(0, 2048)], pick[...], NT)
    a_rest = matmul(
        a_split[:, pl.ds(2048, ROWS - 2048)], pick[pl.ds(0, 128), pl.ds(0, ROWS - 2048)], NT
    )
    place_rows = small(iota((2 * SLOTS, APAD), 0) == a_code)
    rows = [slice(n * APAD, (n + 1) * APAD) for n in range(2)]
    main = sum(matmul(place_rows, a_main[r].astype(BF16), NN) for r in rows)
    rest = sum(matmul(place_rows, a_rest[r].astype(BF16), NN) for r in rows)
    a_msg[:, :, pl.ds(0, 256)] = main.reshape(2, SLOTS, 256)
    a_msg[:, :, pl.ds(256, 128)] = rest.reshape(2, SLOTS, 128)

    pl.semaphore_wait(barrier, 6 + Z * PLACES - 1)

    sends = []

    def send(source, target, send_sem, recv_sem, dd, xx):
        copy = pltpu.make_async_remote_copy(
            src_ref=source,
            dst_ref=target,
            send_sem=send_sem,
            recv_sem=recv_sem,
            device_id=(dd, xx),
            device_id_type=MESH,
        )
        copy.start()
        sends.append(copy)

    for j in range(2):
        cs = core_at[j]
        for m in (2, 1, 3):
            send(
                w_msg.at[2 * x_at[m] + cs],
                w_mid.at[cs, x],
                x_send.at[3 * j + m - 1],
                x_recv.at[cs],
                d,
                x_at[m],
            )
        pltpu.make_async_copy(w_msg.at[2 * x + cs], w_mid.at[cs, x], x_recv.at[cs]).start()

    for m in (3, 1, 2, 0):
        for j in range(2):
            if (m or j) and not (m == 2 and j):
                send(
                    a_msg.at[core_at[j]],
                    a_got.at[place],
                    a_send.at[2 * m + j],
                    a_first if m == 3 and j else a_recv,
                    z * PLACES + y_at[m] * 2 + core_at[j],
                    x,
                )
    pltpu.make_async_copy(a_msg.at[core], a_got.at[place], a_recv).start()

    occ_energy_lane = exact(jnp.broadcast_to(occupied_energy, (8, O)), one_hot(repeat), NN)[:1]
    parts, spread = tiles(slab, (MY // O) * x, 16)
    out_sym = matmul(parts.astype(BF16), small(spread), NN).astype(I32) ^ occ_lane
    parts, _ = tiles(slab_energy, (MY // O) * x, 8)
    out_shift = occ_energy_lane - exact(parts, one_hot(spread), NN)
    out_sym = side_by_side(out_sym, 0, 6)[:, :MY]
    out_shift = side_by_side(out_shift, 0, 6)[:, :MY]

    bj_shift = (
        exact(one_hot(pick_j), jnp.broadcast_to(occupied_energy, (128, O)), NT)
        - exact(one_hot(pick_b), jnp.broadcast_to(slab_energy, (128, n_slab)), NT)
    )[:, :1]
    slot_col = jnp.sum(one_hot(same & (iota(shape, 1) < iota(shape, 0))), axis=1, keepdims=True)
    bj_code_col = jnp.where(bj_sym < 0, -1, 8 * bj_sym + slot_col.astype(I32))

    for j in range(2):
        ready = w_mid.at[core_at[j]]
        pltpu.make_async_copy(ready, ready, x_recv.at[core_at[j]]).wait()
        for n in FAR_FIRST:
            zs = z_at[n]
            if n or j:
                send(
                    ready.at[lax.div(zs, 2), lax.rem(zs, 2)],
                    w_got.at[j, z],
                    w_send.at[j, n],
                    w_recv.at[j],
                    zs * PLACES + here + core_at[j],
                    x,
                )
            else:
                pltpu.make_async_copy(
                    ready.at[lax.div(z, 2), lax.rem(z, 2)], w_got.at[0, z], w_recv.at[0]
                ).start()

    passed = a_got.at[y_at[1] * 2 + core_at[1]]
    pltpu.make_async_copy(passed, passed, a_first).wait()
    send(passed, passed, a_send.at[5], a_recv, z * PLACES + y_at[3] * 2 + core, x)

    a_all[...] = jnp.zeros(a_all.shape, F32)
    others = a_got.at[pl.ds(0, PLACES - 1)]
    pltpu.make_async_copy(others, others, a_recv).wait()
    for p in range(PLACES):
        first = 2 * START[p]
        a_all[pl.ds(first, SLOTS), :] += a_got[p]
    a_high, a_low = halves(a_all[...])
    slot_o = z * PLACES + 2 * x + core

    for j in range(2):
        pltpu.make_async_copy(w_got.at[j], w_got.at[j], w_recv.at[j]).wait()
        rows = []
        for slot in range(8):
            tail = w_got[j, :, 16 + slot % 4, :]
            if slot >= 4:
                tail = pltpu.roll(tail, 64, 1)
            rows.append(
                jnp.concatenate([w_got[j, :, slot, :], w_got[j, :, 8 + slot, :], tail], axis=1)
            )
        w_high, w_low = halves(jnp.concatenate(rows, axis=0))
        product = matmul(w_high, a_low, NN) + matmul(w_low, a_high, NN)
        product = product + matmul(w_high, a_high, NN)
        for part in range(X):
            lanes = product[:, part * QA : (part + 1) * QA]
            ends = []
            for slot in (6, 7):
                whole = lanes[8 * slot : 8 * slot + 8]
                ends.append([whole[:, :40], whole[:, 40:80], whole[:, 80:]])
            nothing = jnp.zeros((8, 32), F32)
            ends = [
                ends[0][0],
                ends[0][1],
                ends[1][0],
                ends[1][1],
                jnp.concatenate([ends[0][2], nothing], axis=1),
                jnp.concatenate([ends[1][2], nothing], axis=1),
            ]
            for slot in range(6):
                o_msg[part, j, :, slot, :] = jnp.concatenate(
                    [lanes[8 * slot : 8 * slot + 8], ends[slot]], axis=1
                )

        for n in FAR_FIRST:
            for m in range(X):
                if n == 4 and j == 0:
                    send(
                        o_msg.at[x_at[m], 0, z_at[n]],
                        o_pass.at[m],
                        o_send.at[0, X * n + m],
                        pass_recv,
                        z_at[7] * PLACES + here + core,
                        x,
                    )
                elif n or m or j:
                    send(
                        o_msg.at[x_at[m], j, z_at[n]],
                        o_got.at[slot_o],
                        o_send.at[j, X * n + m],
                        o_recv,
                        z_at[n] * PLACES + here + core_at[j],
                        x_at[m],
                    )
                else:
                    pltpu.make_async_copy(o_msg.at[x, 0, z], o_got.at[slot_o], o_recv).start()

    pltpu.make_async_copy(o_pass, o_pass, pass_recv).wait()
    for m in range(X):
        send(
            o_pass.at[m],
            o_got.at[z_at[1] * PLACES + 2 * x + core],
            pass_send.at[m],
            o_recv,
            z_at[5] * PLACES + here + core,
            x_at[m],
        )

    o_sum[...] = jnp.zeros(o_sum.shape, F32)
    source = iota((BPAD, 128), 1) & 63
    spread = small(source == bj_code_col)
    end_row = source & 7
    end_slot = jnp.where((end_row == 2) | (end_row == 3) | (end_row == 5), 7, 6)
    end_slot = jnp.where(end_row < 6, end_slot, 8)
    spread_ends = small((source & 56) + end_slot == bj_code_col)
    pltpu.make_async_copy(o_got, o_got, o_recv).wait()
    total = o_got[pl.ds(0, PLACES)]
    for zs in range(1, Z):
        total = total + o_got[pl.ds(zs * PLACES, PLACES)]
    o_sum[:, pl.ds(0, 6), :] = total
    total = o_sum[...].reshape(IRREPS * 8, 128)
    row, lane = iota((IRREPS * 8, 128), 0) & 7, iota((IRREPS * 8, 128), 1)
    first = jnp.where(((row == 0) | (row == 2)) & (lane < 40), pltpu.roll(total, 40, 1), 0.0)
    second = ((row == 1) | (row == 3)) & (lane >= 40) & (lane < 80)
    second = jnp.where(second, pltpu.roll(total, 80, 1), 0.0)
    third = ((row == 4) | (row == 5)) & (lane >= 80) & (lane < QA)
    third = jnp.where(third, pltpu.roll(total, 120, 1), 0.0)
    high, low = halves(total)
    mine = matmul(spread, jnp.concatenate([high, low], axis=0), NN)
    high, low = halves(first + second + third)
    mine = mine + matmul(spread_ends, jnp.concatenate([high, low], axis=0), NN)
    high, low = halves(mine)
    widen = pick[pl.ds(0, 128), pl.ds(0, MY)]
    cycle = matmul(high, widen, NN) + matmul(low, widen, NN)
    value = jnp.where(bj_sym == out_sym, cycle, 0.0) / (out_shift + bj_shift)
    out_ref[...] = value[:BJ]

    for copy in sends:
        copy.wait_send()


def local(
    amplitudes, integrals, slab_irrep, virtual_irrep, occupied_irrep, occupied_energy, slab_energy
):
    vmem = pl.BlockSpec(memory_space=pltpu.VMEM)
    hbm = pl.BlockSpec(memory_space=pltpu.HBM)
    out = pl.pallas_call(
        kernel,
        out_shape=jax.ShapeDtypeStruct((BJ, MY), F32),
        in_specs=[hbm] * 7,
        out_specs=vmem,
        scratch_shapes=[
            pltpu.VMEM(slab_irrep.shape, I32),
            pltpu.VMEM(virtual_irrep.shape, I32),
            pltpu.VMEM(occupied_irrep.shape, I32),
            pltpu.VMEM(occupied_energy.shape, F32),
            pltpu.VMEM(slab_energy.shape, F32),
            pltpu.VMEM((COLS, ROWS), F32),
            pltpu.VMEM((BJ, WIDE), F32),
            pltpu.VMEM((2 * APAD, ROWS), BF16),
            pltpu.VMEM((4 * BPAD, 2432), BF16),
            pltpu.VMEM((256, 2048), BF16),
            pltpu.VMEM((2, SLOTS, 384), F32),
            pltpu.VMEM((IRREPS, 2, 20, 128), F32),
            pltpu.VMEM((2, X, 2, 20, 128), F32),
            pltpu.VMEM((PLACES, SLOTS, 384), F32),
            pltpu.VMEM((2, Z, 20, 128), F32),
            pltpu.VMEM((384, 384), F32),
            pltpu.VMEM((1, 38 * 128), I32),
            pltpu.VMEM((X, 2, Z, 6, 128), F32),
            pltpu.VMEM((X, 6, 128), F32),
            pltpu.VMEM((Z * PLACES, 6, 128), F32),
            pltpu.VMEM((IRREPS, 8, 128), F32),
            pltpu.SemaphoreType.DMA((7,)),
            pltpu.SemaphoreType.DMA((PLACES,)),
            pltpu.SemaphoreType.DMA((6,)),
            pltpu.SemaphoreType.DMA((2, Z)),
            pltpu.SemaphoreType.DMA((2, Z * X)),
            pltpu.SemaphoreType.DMA,
            pltpu.SemaphoreType.DMA,
            pltpu.SemaphoreType.DMA((2,)),
            pltpu.SemaphoreType.DMA((2,)),
            pltpu.SemaphoreType.DMA,
            pltpu.SemaphoreType.DMA((X,)),
            pltpu.SemaphoreType.DMA,
        ],
        compiler_params=pltpu.CompilerParams(
            collective_id=0, has_side_effects=True, vmem_limit_bytes=58 << 20
        ),
    )(
        amplitudes.T,
        integrals,
        slab_irrep,
        virtual_irrep,
        occupied_irrep,
        occupied_energy,
        slab_energy,
    )
    return out.T


def solution(mesh):
    return jax.shard_map(
        local,
        mesh=mesh,
        in_specs=(P(None, "dist"), P("dist", "rep"), P(), P(), P(), P(), P()),
        out_specs=P("rep", "dist"),
        check_vma=False,
    )
```

```python
import jax
import jax.numpy as jnp
from jax import lax
from jax.experimental import pallas as pl
from jax.experimental.pallas import tpu as pltpu
from jax.sharding import PartitionSpec as P

MESH = pl.DeviceIdType.MESH
F32, BF16, I32 = jnp.float32, jnp.bfloat16, jnp.int32

O = 16
IRREPS = 8
Z, Y, X = 8, 4, 4
PLACES = 8
ROWS = 2816
COLS = 300
WIDE = 4800
HALF = 2400
BJ = 44
MY = 704
SLOTS = 40
QA = 88
APAD, BPAD = 304, 48
START = [(COLS * p) // O for p in range(PLACES)]


def halves(value):
    high = value.astype(BF16)
    return high, (value - high.astype(F32)).astype(BF16)


def matmul(left, right, dims):
    return lax.dot_general(left, right, (dims, ((), ())), preferred_element_type=F32)


NN = ((1,), (0,))
NT = ((1,), (1,))


def iota(shape, dim):
    return lax.broadcasted_iota(I32, shape, dim)


def exact(left, right, dims):
    return lax.dot_general(
        left, right, (dims, ((), ())), precision=lax.Precision.HIGHEST, preferred_element_type=F32
    )


def one_hot(mask):
    return mask.astype(F32)


def small(mask):
    return mask.astype(F32).astype(BF16)


def tiles(values, offset, count):
    size = values.shape[1]
    at = iota((count, size), 1) - offset
    parts = jnp.where((at >> 3) == iota((count, size), 0), values, 0.0)
    spread = ((iota((size, 128), 0) - offset) & 7) == (iota((size, 128), 1) >> 4)
    return parts, spread


FAR_FIRST = (4, 5, 3, 6, 2, 7, 1, 0)


def side_by_side(rows, first, count):
    return jnp.concatenate([rows[first + n : first + n + 1] for n in range(count)], axis=1)


def kernel(
    a_hbm,
    w_hbm,
    slab_hbm,
    virtual_hbm,
    occupied_hbm,
    occupied_energy_hbm,
    slab_energy_hbm,
    out_ref,
    slab_ref,
    virtual_ref,
    occupied_ref,
    occupied_energy_ref,
    slab_energy_ref,
    a_in,
    w_in,
    a_split,
    w_split,
    pick,
    a_msg,
    w_msg,
    w_mid,
    a_got,
    w_got,
    a_all,
    w_sym,
    o_msg,
    o_pass,
    o_got,
    o_sum,
    load_sem,
    a_send,
    x_send,
    w_send,
    o_send,
    a_first,
    a_recv,
    x_recv,
    w_recv,
    o_recv,
    pass_send,
    pass_recv,
):
    d = lax.axis_index("dist")
    x = lax.axis_index("rep")
    z, place = lax.div(d, PLACES), lax.rem(d, PLACES)
    y, core = lax.div(place, 2), lax.rem(place, 2)
    z_at = [lax.rem(z + n, Z) for n in range(Z)]
    y_at = [lax.rem(y + n, Y) for n in range(Y)]
    x_at = [lax.rem(x + n, X) for n in range(X)]
    core_at = [core, 1 - core]
    here = y * 2
    load_a = pltpu.make_async_copy(a_hbm, a_in, load_sem.at[0])
    load_w = pltpu.make_async_copy(w_hbm, w_in, load_sem.at[1])
    loads = [
        pltpu.make_async_copy(source, target, load_sem.at[2 + n])
        for n, (source, target) in enumerate(
            [
                (occupied_hbm, occupied_ref),
                (slab_hbm, slab_ref),
                (virtual_hbm, virtual_ref),
                (occupied_energy_hbm, occupied_energy_ref),
                (slab_energy_hbm, slab_energy_ref),
            ]
        )
    ]
    for load in loads:
        load.start()
    load_w.start()
    load_a.start()

    barrier = pltpu.get_barrier_semaphore()

    def greet(dd, xx):
        pl.semaphore_signal(barrier, inc=1, device_id=(dd, xx), device_id_type=MESH)

    for n in FAR_FIRST:
        for m in range(X):
            for j in range(2):
                if n or m or j:
                    greet(z_at[n] * PLACES + here + core_at[j], x_at[m])
    for m in range(1, Y):
        for j in range(2):
            greet(z * PLACES + y_at[m] * 2 + core_at[j], x)

    for load in loads:
        load.wait()
    slab = slab_ref[...].reshape(1, -1).astype(F32)
    virtual = virtual_ref[...].reshape(1, -1).astype(F32)
    occupied = occupied_ref[...].reshape(1, -1).astype(F32)
    occupied_energy = occupied_energy_ref[...].reshape(1, -1)
    slab_energy = slab_energy_ref[...].reshape(1, -1)
    n_slab, n_virtual = slab.shape[1], virtual.shape[1]
    slab_all = jnp.broadcast_to(slab, (128, n_slab)).astype(BF16)
    occ_all = jnp.broadcast_to(occupied, (128, O)).astype(BF16)

    repeat = iota((O, 128), 0) == (iota((O, 128), 1) & 15)
    occ_lane = matmul(occ_all[:16], small(repeat), NN)[:1].astype(I32)
    occ_col = matmul(small(iota((O, O), 0) == iota((O, O), 1)), occ_all, NT).astype(I32)
    earlier = (occ_col == occ_lane) & (iota((O, 128), 0) < (iota((O, 128), 1) & 15))
    rank = jnp.sum(one_hot(earlier), axis=0, keepdims=True)
    key = 2 * (iota((1, 128), 1) >> 4) + rank.astype(I32)

    parts, spread = tiles(slab, 0, 32)
    row_sym = matmul(parts.astype(BF16), small(spread), NN).astype(I32) ^ occ_lane
    parts, spread = tiles(virtual, (WIDE // O) * x, 48)
    columns = matmul(parts.astype(BF16), small(spread), NN).astype(I32) ^ occ_lane
    for n in range(38):
        w_sym[:, pl.ds(n * 128, 128)] = columns[n : n + 1]

    first_c, inside = (COLS * d) // O, (COLS * d) % O
    near = small(iota((n_virtual, 128), 0) == first_c + iota((n_virtual, 128), 1))
    near = matmul(jnp.broadcast_to(virtual, (16, n_virtual)).astype(BF16), near, NN)
    near_all = jnp.broadcast_to(near[:1], (128, 128)).astype(BF16)
    at = inside + iota((APAD, 128), 0)
    v_col = matmul(small((at >> 4) == iota((APAD, 128), 1)), near_all, NT).astype(I32)
    at = inside + iota((APAD, O), 0)
    o_col = matmul(small((at & 15) == iota((APAD, O), 1)), occ_all, NT).astype(I32)
    a_col_sym = (v_col ^ o_col)[:COLS, :1]
    at = inside + iota((128, 384), 1)
    v_row = matmul(near_all[:16], small((at >> 4) == iota((128, 384), 0)), NN)[:1].astype(I32)
    at = inside + iota((O, 384), 1)
    pick_o = small((at & 15) == iota((O, 384), 0))
    o_row = matmul(occ_all[:16], pick_o, NN)[:1].astype(I32)
    rank_all = jnp.broadcast_to(rank[:, :O], (16, O)).astype(BF16)
    rank_row = matmul(rank_all, pick_o, NN)[:1].astype(I32)
    at = inside + iota((1, 384), 1)
    a_code = SLOTS * ((v_row ^ o_row) - 2 * x) + 2 * (at >> 4) + rank_row
    a_code = jnp.where(iota((1, 384), 1) < COLS, a_code, -1)[:, :APAD]

    at = BJ * d + iota((BPAD, n_slab), 0)
    pick_b = (at >> 4) == iota((BPAD, n_slab), 1)
    at = BJ * d + iota((BPAD, O), 0)
    pick_j = (at & 15) == iota((BPAD, O), 1)
    bj_col = matmul(small(pick_b), slab_all, NT).astype(I32) ^ matmul(
        small(pick_j), occ_all, NT
    ).astype(I32)
    bj_sym = jnp.where(iota((BPAD, 128), 0) < BJ, bj_col, -1)
    at = BJ * d + iota((n_slab, 128), 1)
    b_row = matmul(slab_all[:16], small((at >> 4) == iota((n_slab, 128), 0)), NN)[:1]
    at = BJ * d + iota((O, 128), 1)
    j_row = matmul(occ_all[:16], small((at & 15) == iota((O, 128), 0)), NN)[:1]
    bj_row = jnp.where(iota((1, 128), 1) < BJ, b_row.astype(I32) ^ j_row.astype(I32), -1)
    same = bj_sym == bj_row
    shape = (BPAD, 128)
    slot_row = jnp.sum(one_hot(same & (iota(shape, 0) < iota(shape, 1))), axis=0, keepdims=True)
    bj_code = jnp.where(bj_row < 0, -1, 8 * bj_row + slot_row.astype(I32))[:, :BPAD]
    bj_sym = bj_sym[:, :1]

    pick[...] = jnp.zeros(pick.shape, BF16)
    one_tile = small(key == iota((16, 128), 0))
    for n in range(16):
        pick[pl.ds(16 * n, 16), pl.ds(n * 128, 128)] = one_tile
    for n in range(4):
        w_split[pl.ds(n * BPAD + 32, 16)] = jnp.zeros((16, 2432), BF16)
    for n in range(2):
        a_split[pl.ds(n * APAD + 288, 16)] = jnp.zeros((16, ROWS), BF16)

    load_w.wait()
    for half in range(2):
        cols = pl.ds(half * HALF, HALF)
        kept = jnp.where(bj_sym[:BJ] == w_sym[:, cols], w_in[:, cols], 0.0)
        high, low = halves(kept)
        w_split[pl.ds(half * 2 * BPAD, BJ), pl.ds(0, HALF)] = high
        w_split[pl.ds((half * 2 + 1) * BPAD, BJ), pl.ds(0, HALF)] = low
    w_main = matmul(w_split[:, pl.ds(0, 2048)], pick[...], NT)
    w_rest = matmul(
        w_split[:, pl.ds(2048, HALF - 2048)], pick[pl.ds(0, 128), pl.ds(0, HALF - 2048)], NT
    )
    row = iota((IRREPS * 8, BPAD), 0)
    group = small(row == bj_code)
    row = row & 31
    row = 8 * (row >> 2) + (row & 3) + 4 * (iota((IRREPS * 8, BPAD), 0) >> 5)
    group_rest = small(row == bj_code)
    for half in range(2):
        rows = [slice((2 * half + n) * BPAD, (2 * half + n + 1) * BPAD) for n in range(2)]
        main = sum(matmul(group, w_main[r].astype(BF16), NN) for r in rows)
        rest = sum(matmul(group_rest, w_rest[r].astype(BF16), NN) for r in rows)
        w_msg[:, half, pl.ds(0, 8)] = main[:, :128].reshape(IRREPS, 8, 128)
        w_msg[:, half, pl.ds(8, 8)] = main[:, 128:].reshape(IRREPS, 8, 128)
        rest = rest[:32] + pltpu.roll(rest[32:], 64, 1)
        w_msg[:, half, pl.ds(16, 4)] = rest.reshape(IRREPS, 4, 128)

    load_a.wait()
    for n in range(11):
        cols = pl.ds(n * 256, 256)
        kept = jnp.where(
            a_col_sym == side_by_side(row_sym, 2 * n, 2), a_in[:, cols], 0.0
        )
        high, low = halves(kept)
        a_split[pl.ds(0, COLS), cols] = high
        a_split[pl.ds(APAD, COLS), cols] = low
    a_main = matmul(a_split[:, pl.ds(0, 2048)], pick[...], NT)
    a_rest = matmul(
        a_split[:, pl.ds(2048, ROWS - 2048)], pick[pl.ds(0, 128), pl.ds(0, ROWS - 2048)], NT
    )
    place_rows = small(iota((2 * SLOTS, APAD), 0) == a_code)
    rows = [slice(n * APAD, (n + 1) * APAD) for n in range(2)]
    main = sum(matmul(place_rows, a_main[r].astype(BF16), NN) for r in rows)
    rest = sum(matmul(place_rows, a_rest[r].astype(BF16), NN) for r in rows)
    a_msg[:, :, pl.ds(0, 256)] = main.reshape(2, SLOTS, 256)
    a_msg[:, :, pl.ds(256, 128)] = rest.reshape(2, SLOTS, 128)

    pl.semaphore_wait(barrier, 6 + Z * PLACES - 1)

    sends = []

    def send(source, target, send_sem, recv_sem, dd, xx):
        copy = pltpu.make_async_remote_copy(
            src_ref=source,
            dst_ref=target,
            send_sem=send_sem,
            recv_sem=recv_sem,
            device_id=(dd, xx),
            device_id_type=MESH,
        )
        copy.start()
        sends.append(copy)

    for j in range(2):
        cs = core_at[j]
        for m in (2, 1, 3):
            send(
                w_msg.at[2 * x_at[m] + cs],
                w_mid.at[cs, x],
                x_send.at[3 * j + m - 1],
                x_recv.at[cs],
                d,
                x_at[m],
            )
        pltpu.make_async_copy(w_msg.at[2 * x + cs], w_mid.at[cs, x], x_recv.at[cs]).start()

    for m in (3, 1, 2, 0):
        for j in range(2):
            if (m or j) and not (m == 2 and j):
                send(
                    a_msg.at[core_at[j]],
                    a_got.at[place],
                    a_send.at[2 * m + j],
                    a_first if m == 3 and j else a_recv,
                    z * PLACES + y_at[m] * 2 + core_at[j],
                    x,
                )
    pltpu.make_async_copy(a_msg.at[core], a_got.at[place], a_recv).start()

    occ_energy_lane = exact(jnp.broadcast_to(occupied_energy, (8, O)), one_hot(repeat), NN)[:1]
    parts, spread = tiles(slab, (MY // O) * x, 16)
    out_sym = matmul(parts.astype(BF16), small(spread), NN).astype(I32) ^ occ_lane
    parts, _ = tiles(slab_energy, (MY // O) * x, 8)
    out_shift = occ_energy_lane - exact(parts, one_hot(spread), NN)
    out_sym = side_by_side(out_sym, 0, 6)[:, :MY]
    out_shift = side_by_side(out_shift, 0, 6)[:, :MY]

    bj_shift = (
        exact(one_hot(pick_j), jnp.broadcast_to(occupied_energy, (128, O)), NT)
        - exact(one_hot(pick_b), jnp.broadcast_to(slab_energy, (128, n_slab)), NT)
    )[:, :1]
    slot_col = jnp.sum(one_hot(same & (iota(shape, 1) < iota(shape, 0))), axis=1, keepdims=True)
    bj_code_col = jnp.where(bj_sym < 0, -1, 8 * bj_sym + slot_col.astype(I32))

    for j in range(2):
        ready = w_mid.at[core_at[j]]
        pltpu.make_async_copy(ready, ready, x_recv.at[core_at[j]]).wait()
        for n in FAR_FIRST:
            zs = z_at[n]
            if n or j:
                send(
                    ready.at[lax.div(zs, 2), lax.rem(zs, 2)],
                    w_got.at[j, z],
                    w_send.at[j, n],
                    w_recv.at[j],
                    zs * PLACES + here + core_at[j],
                    x,
                )
            else:
                pltpu.make_async_copy(
                    ready.at[lax.div(z, 2), lax.rem(z, 2)], w_got.at[0, z], w_recv.at[0]
                ).start()

    passed = a_got.at[y_at[1] * 2 + core_at[1]]
    pltpu.make_async_copy(passed, passed, a_first).wait()
    send(passed, passed, a_send.at[5], a_recv, z * PLACES + y_at[3] * 2 + core, x)

    a_all[...] = jnp.zeros(a_all.shape, F32)
    others = a_got.at[pl.ds(0, PLACES - 1)]
    pltpu.make_async_copy(others, others, a_recv).wait()
    for p in range(PLACES):
        first = 2 * START[p]
        a_all[pl.ds(first, SLOTS), :] += a_got[p]
    a_high, a_low = halves(a_all[...])
    slot_o = z * PLACES + 2 * x + core

    for j in range(2):
        pltpu.make_async_copy(w_got.at[j], w_got.at[j], w_recv.at[j]).wait()
        rows = []
        for slot in range(8):
            tail = w_got[j, :, 16 + slot % 4, :]
            if slot >= 4:
                tail = pltpu.roll(tail, 64, 1)
            rows.append(
                jnp.concatenate([w_got[j, :, slot, :], w_got[j, :, 8 + slot, :], tail], axis=1)
            )
        w_high, w_low = halves(jnp.concatenate(rows, axis=0))
        product = matmul(w_high, a_low, NN) + matmul(w_low, a_high, NN)
        product = product + matmul(w_high, a_high, NN)
        for part in range(X):
            lanes = product[:, part * QA : (part + 1) * QA]
            ends = []
            for slot in (6, 7):
                whole = lanes[8 * slot : 8 * slot + 8]
                ends.append([whole[:, :40], whole[:, 40:80], whole[:, 80:]])
            nothing = jnp.zeros((8, 32), F32)
            ends = [
                ends[0][0],
                ends[0][1],
                ends[1][0],
                ends[1][1],
                jnp.concatenate([ends[0][2], nothing], axis=1),
                jnp.concatenate([ends[1][2], nothing], axis=1),
            ]
            for slot in range(6):
                o_msg[part, j, :, slot, :] = jnp.concatenate(
                    [lanes[8 * slot : 8 * slot + 8], ends[slot]], axis=1
                )

        for n in FAR_FIRST:
            for m in range(X):
                if n == 4 and j == 0:
                    send(
                        o_msg.at[x_at[m], 0, z_at[n]],
                        o_pass.at[m],
                        o_send.at[0, X * n + m],
                        pass_recv,
                        z_at[6] * PLACES + here + core,
                        x,
                    )
                elif n or m or j:
                    send(
                        o_msg.at[x_at[m], j, z_at[n]],
                        o_got.at[slot_o],
                        o_send.at[j, X * n + m],
                        o_recv,
                        z_at[n] * PLACES + here + core_at[j],
                        x_at[m],
                    )
                else:
                    pltpu.make_async_copy(o_msg.at[x, 0, z], o_got.at[slot_o], o_recv).start()

    pltpu.make_async_copy(o_pass, o_pass, pass_recv).wait()
    for m in range(X):
        send(
            o_pass.at[m],
            o_got.at[z_at[2] * PLACES + 2 * x + core],
            pass_send.at[m],
            o_recv,
            z_at[6] * PLACES + here + core,
            x_at[m],
        )

    o_sum[...] = jnp.zeros(o_sum.shape, F32)
    source = iota((BPAD, 128), 1) & 63
    spread = small(source == bj_code_col)
    end_row = source & 7
    end_slot = jnp.where((end_row == 2) | (end_row == 3) | (end_row == 5), 7, 6)
    end_slot = jnp.where(end_row < 6, end_slot, 8)
    spread_ends = small((source & 56) + end_slot == bj_code_col)
    pltpu.make_async_copy(o_got, o_got, o_recv).wait()
    total = o_got[pl.ds(0, PLACES)]
    for zs in range(1, Z):
        total = total + o_got[pl.ds(zs * PLACES, PLACES)]
    o_sum[:, pl.ds(0, 6), :] = total
    total = o_sum[...].reshape(IRREPS * 8, 128)
    row, lane = iota((IRREPS * 8, 128), 0) & 7, iota((IRREPS * 8, 128), 1)
    first = jnp.where(((row == 0) | (row == 2)) & (lane < 40), pltpu.roll(total, 40, 1), 0.0)
    second = ((row == 1) | (row == 3)) & (lane >= 40) & (lane < 80)
    second = jnp.where(second, pltpu.roll(total, 80, 1), 0.0)
    third = ((row == 4) | (row == 5)) & (lane >= 80) & (lane < QA)
    third = jnp.where(third, pltpu.roll(total, 120, 1), 0.0)
    high, low = halves(total)
    mine = matmul(spread, jnp.concatenate([high, low], axis=0), NN)
    high, low = halves(first + second + third)
    mine = mine + matmul(spread_ends, jnp.concatenate([high, low], axis=0), NN)
    high, low = halves(mine)
    widen = pick[pl.ds(0, 128), pl.ds(0, MY)]
    cycle = matmul(high, widen, NN) + matmul(low, widen, NN)
    value = jnp.where(bj_sym == out_sym, cycle, 0.0) / (out_shift + bj_shift)
    out_ref[...] = value[:BJ]

    for copy in sends:
        copy.wait_send()


def local(
    amplitudes, integrals, slab_irrep, virtual_irrep, occupied_irrep, occupied_energy, slab_energy
):
    vmem = pl.BlockSpec(memory_space=pltpu.VMEM)
    hbm = pl.BlockSpec(memory_space=pltpu.HBM)
    out = pl.pallas_call(
        kernel,
        out_shape=jax.ShapeDtypeStruct((BJ, MY), F32),
        in_specs=[hbm] * 7,
        out_specs=vmem,
        scratch_shapes=[
            pltpu.VMEM(slab_irrep.shape, I32),
            pltpu.VMEM(virtual_irrep.shape, I32),
            pltpu.VMEM(occupied_irrep.shape, I32),
            pltpu.VMEM(occupied_energy.shape, F32),
            pltpu.VMEM(slab_energy.shape, F32),
            pltpu.VMEM((COLS, ROWS), F32),
            pltpu.VMEM((BJ, WIDE), F32),
            pltpu.VMEM((2 * APAD, ROWS), BF16),
            pltpu.VMEM((4 * BPAD, 2432), BF16),
            pltpu.VMEM((256, 2048), BF16),
            pltpu.VMEM((2, SLOTS, 384), F32),
            pltpu.VMEM((IRREPS, 2, 20, 128), F32),
            pltpu.VMEM((2, X, 2, 20, 128), F32),
            pltpu.VMEM((PLACES, SLOTS, 384), F32),
            pltpu.VMEM((2, Z, 20, 128), F32),
            pltpu.VMEM((384, 384), F32),
            pltpu.VMEM((1, 38 * 128), I32),
            pltpu.VMEM((X, 2, Z, 6, 128), F32),
            pltpu.VMEM((X, 6, 128), F32),
            pltpu.VMEM((Z * PLACES, 6, 128), F32),
            pltpu.VMEM((IRREPS, 8, 128), F32),
            pltpu.SemaphoreType.DMA((7,)),
            pltpu.SemaphoreType.DMA((PLACES,)),
            pltpu.SemaphoreType.DMA((6,)),
            pltpu.SemaphoreType.DMA((2, Z)),
            pltpu.SemaphoreType.DMA((2, Z * X)),
            pltpu.SemaphoreType.DMA,
            pltpu.SemaphoreType.DMA,
            pltpu.SemaphoreType.DMA((2,)),
            pltpu.SemaphoreType.DMA((2,)),
            pltpu.SemaphoreType.DMA,
            pltpu.SemaphoreType.DMA((X,)),
            pltpu.SemaphoreType.DMA,
        ],
        compiler_params=pltpu.CompilerParams(
            collective_id=0, has_side_effects=True, vmem_limit_bytes=58 << 20
        ),
    )(
        amplitudes.T,
        integrals,
        slab_irrep,
        virtual_irrep,
        occupied_irrep,
        occupied_energy,
        slab_energy,
    )
    return out.T


def solution(mesh):
    return jax.shard_map(
        local,
        mesh=mesh,
        in_specs=(P(None, "dist"), P("dist", "rep"), P(), P(), P(), P(), P()),
        out_specs=P("rep", "dist"),
        check_vma=False,
    )
```
